128 devices in a mesh: wide: 16 (over x, y_lo, core), narrow: 8 (over z, y_hi).
Axes of the slice: x: 4, y: 4 (y_hi: 2, y_lo: 2; y = y_hi * 2 + y_lo), z: 4, core: 2. Of those that a mesh axis runs over, the one named last changes fastest.
Arguments:
- positions: float32 [2, 1048576], P(None, ('wide', 'narrow')), may hold values from -1 to 1
- angles: float32 [1048576], P(('wide', 'narrow')), may hold values from -3.140625 to 3.140625
- weights: float32 [1048576], P(('wide', 'narrow')), may hold values from -6 to 6
- owner_dev: int32 [1048576, 1], P(('wide', 'narrow')), may hold values from 0 to 127; in each aligned block of 8192 rows (0 to 8191, 8192 to 16383, ...) at most 256 rows name the same one
- leaf_slot: int32 [1048576], P(('wide', 'narrow')), may hold values from 0 to 255
- phase_table: float32 [5, 32768, 256], P(None, ('wide', 'narrow')), may hold values from -3.140625 to 3.140625
Outputs:
- radon_field: float32 [32768, 512], P(('wide', 'narrow'))
The draws below stay inside these ranges and needn't reach their ends.
Inputs may be any that keep to these rules, and one draw needn't show every extreme that they name: `owner_dev`: among the rows of one device no owner is named more than 256 times, and in every draw some owner is named exactly 256 times by the rows of some device.
All inputs are finite; a program needn't handle non-finite values.
Results may differ from the reference program's by a relative error of at most 0.0003.
Values sent between devices are 32-bit elements; how exact they have to be, the bound alone decides.
A program may use at most 128 MiB of HBM per device.

```python
import math
import jax
import jax.numpy as jnp
import numpy as np
from jax import lax

Q = 16
LEVELS = 5
SRC_DEV = 8192
BOX_DEV = 256
SOURCES = 1048576
BOXES = 32768
CAP = 256
N_WIDE = 16
N_NARROW = 8
DEVICES = 128


def with_ends(entries, rng, low, top_value):
    dims = entries.shape
    place = [jax.random.randint(jax.random.fold_in(rng, axis), (), 0, dims[axis]) for axis in range(len(dims))]
    entries = entries.at[tuple(place)].set(low)
    longest = dims.index(max(dims))
    place[longest] = (place[longest] + 1) % dims[longest]
    return entries.at[tuple(place)].set(top_value)


def block_levels(own_key, extent, cuts, low, largest):
    loudness = 1.0
    for axis_at, shards_of in cuts:
        steps = jax.random.uniform(jax.random.fold_in(jax.random.fold_in(own_key, 6), axis_at), (shards_of,), jnp.float32, low / len(cuts), largest / len(cuts))
        loudness = loudness * jnp.repeat(jnp.exp(steps), extent[axis_at] // shards_of).reshape((-1,) + (1,) * (len(extent) - 1 - axis_at))
    return loudness


def deal_out(own_key, own, number, rows, count, top, most, slope):
    order = jax.random.permutation(own_key, count)
    heavy_load, ordinary = portions_of(count, rows * top, most, slope, True), portions_of(count, rows * top, most, slope, False)
    places = jnp.arange(count)

    def named(sizes, offset_by):
        used = int((sizes > 0).sum())
        fixed = max(1, used // 4)
        passed = fixed + (places - fixed + offset_by * (used - fixed)) % max(1, count - fixed)
        return jnp.zeros((count,), jnp.int32).at[order[jnp.where(places < fixed, places, passed)]].set(jnp.asarray(sizes, jnp.int32))

    sizes = jnp.where(number % 4 == 0, named(heavy_load, number // 4), named(ordinary, number - number // 4 - 1))
    mixed = jax.random.permutation(jax.random.fold_in(own, 3), count)
    source_of, sink = mixed[0:count // 2 * 2:2], mixed[1:count // 2 * 2:2]
    slack = jnp.minimum(sizes[source_of] - 1, most - sizes[sink]) // 2
    slack = jnp.where((source_of == order[0]) | (sink == order[0]) | (sizes[sink] == 0), 0, jnp.maximum(slack, 0))
    passed = jax.random.randint(jax.random.fold_in(own, 4), (count // 2,), 0, 1 << 20) % (slack + 1)
    sizes = sizes.at[source_of].add(-passed).at[sink].add(passed)
    items = jnp.searchsorted(jnp.cumsum(sizes), jnp.arange(rows * top), side="right").astype(jnp.int32)
    grid = items.reshape(top, rows).T
    grid = grid[jax.random.permutation(jax.random.fold_in(own, 1), rows)]
    offset_by = jax.random.randint(jax.random.fold_in(own, 2), (rows, 1), 0, top)
    return jnp.take_along_axis(grid, (jnp.arange(top)[None, :] + offset_by) % top, axis=1)


def portions_of(number_of, total, most, skew, full):
    loads = [(1 << 20) // math.isqrt(standing ** skew) + 1 for standing in range(1, number_of + 1)]
    largest = most if full else min(most, max(-(-total // number_of), total * loads[0] // sum(loads)))
    least = 1 if total - largest >= number_of - 1 else 0
    given, rest = [largest] + [least] * (number_of - 1), total - largest - least * (number_of - 1)
    while rest > 0:
        candidates = [i for i in range(1, number_of) if given[i] < largest] or [i for i in range(1, number_of) if given[i] < most]
        mass, budget = sum([loads[i] for i in candidates]), rest
        for i in candidates:
            addition = min(most - given[i], max(1, budget * loads[i] // mass), rest)
            given[i] = given[i] + addition
            rest = rest - addition
    return np.array(given)


def normal_values(stream_key, shape, deviation, reach, cuts=(), held_as=jnp.bfloat16):
    array = jax.random.normal(stream_key, shape, jnp.float32) * deviation
    if len(cuts) > 0:
        array = block_levels(stream_key, shape, cuts, -0.22, 0.18) * array
    return jnp.clip(array, min=-reach, max=reach).astype(held_as)


def setup_inputs(seed: int = 0) -> dict:
    arg_keys = jax.random.split(jax.random.key(seed), 7)
    positions = jnp.clip(jax.random.uniform(arg_keys[0], (2, SOURCES), jnp.float32, -1.0, 1.0) * block_levels(arg_keys[0], (2, SOURCES), ((1, 128),), -0.4, 0.0), -1.0, 1.0)
    angles = jnp.clip(jax.random.uniform(arg_keys[1], (SOURCES,), jnp.float32, -3.140625, 3.140625), -3.140625, 3.140625)
    weights = normal_values(arg_keys[2], (SOURCES,), 1.0, 6.0, ((0, 128),), jnp.float32)
    owner_dev_keys = jax.random.split(jax.random.fold_in(arg_keys[3], 1), SOURCES // SRC_DEV)
    owner_dev_turns = jax.random.permutation(jax.random.fold_in(arg_keys[3], 3), SOURCES // SRC_DEV)
    owner_dev = jax.vmap(lambda own, number: deal_out(jax.random.fold_in(arg_keys[3], 2), own, number, SRC_DEV, DEVICES, 1, CAP, 2))(owner_dev_keys, owner_dev_turns).reshape((SOURCES, 1))
    leaf_slot = with_ends(jax.random.randint(arg_keys[4], (SOURCES,), 0, BOX_DEV), jax.random.fold_in(arg_keys[4], 1), 0, BOX_DEV - 1).astype(jnp.int32)
    phase_table = jnp.clip(jax.random.uniform(arg_keys[5], (LEVELS, BOXES, Q * Q), jnp.float32, -3.140625, 3.140625), -3.140625, 3.140625)
    return {"positions": positions, "angles": angles, "weights": weights, "owner_dev": owner_dev, "leaf_slot": leaf_slot, "phase_table": phase_table}


LEAF_GAIN = 5.0
SQRT_HALF = 0.7071067811865476
HIGH = lax.Precision.HIGHEST


def cheb_nodes(grid_order):
    counter = jnp.arange(grid_order, dtype=jnp.float32)
    return jnp.cos((2.0 * counter + 1.0) * math.pi / (2.0 * grid_order))


def lagrange(points, grid_order):
    node_list = cheb_nodes(grid_order)
    offsets = points[..., None] - node_list
    unit_col = jnp.ones_like(offsets[..., :1])
    before = jnp.cumprod(jnp.concatenate([unit_col, offsets[..., :-1]], -1), -1)
    after_prod = jnp.flip(jnp.cumprod(jnp.concatenate([unit_col, jnp.flip(offsets[..., 1:], -1)], -1), -1), -1)
    node_gaps = node_list[:, None] - node_list[None, :] + jnp.eye(grid_order, dtype=jnp.float32)
    node_prod = jnp.prod(node_gaps, 1)
    return before * after_prod / node_prod


def interp_kron(grid_order, side_value):
    node_list = cheb_nodes(grid_order)
    interp = lagrange((node_list + (2.0 * side_value - 1.0)) * 0.5, grid_order)
    return (interp[:, None, :, None] * interp[None, :, None, :]).reshape(grid_order * grid_order, grid_order * grid_order)


def apply_kron(coeffs, kron_matrix):
    flat_rows = coeffs.reshape(-1, kron_matrix.shape[0])
    result = lax.dot_general(flat_rows, kron_matrix, (((1,), (1,)), ((), ())), precision=HIGH, preferred_element_type=jnp.float32)
    return result.reshape(coeffs.shape)


def rotate(coeffs, angle_rows):
    half_width = angle_rows.shape[-1]
    real_part = coeffs[..., :half_width]
    imag_part = coeffs[..., half_width:]
    cosine = jnp.cos(angle_rows)
    sine_val = jnp.sin(angle_rows)
    return jnp.concatenate([cosine * real_part - sine_val * imag_part, sine_val * real_part + cosine * imag_part], -1)


def leaf_terms(first_pos, second_pos, phase_angle, weight, grid_order):
    first_basis = lagrange(first_pos, grid_order)
    second_basis = lagrange(second_pos, grid_order)
    outer_prod = (first_basis[:, :, None] * second_basis[:, None, :]).reshape(-1, grid_order * grid_order) * (LEAF_GAIN * weight)[:, None]
    return jnp.concatenate([outer_prod * jnp.cos(phase_angle)[:, None], outer_prod * jnp.sin(phase_angle)[:, None]], 1)


def reference(positions, angles, weights, owner_dev, leaf_slot, phase_table):
    points_sq = Q * Q
    box_ids = (owner_dev[:, 0] * BOX_DEV + leaf_slot).astype(jnp.int32)
    block_rows = math.gcd(SOURCES, 16384)

    def add_block(block_no, running):
        start = (block_no * block_rows).astype(jnp.int32)
        first_pos = lax.dynamic_slice_in_dim(positions[0], start, block_rows)
        second_pos = lax.dynamic_slice_in_dim(positions[1], start, block_rows)
        block_angle = lax.dynamic_slice_in_dim(angles, start, block_rows)
        block_weight = lax.dynamic_slice_in_dim(weights, start, block_rows)
        block_ids = lax.dynamic_slice_in_dim(box_ids, start, block_rows)
        term_rows = leaf_terms(first_pos, second_pos, block_angle, block_weight, Q)
        return running + jax.ops.segment_sum(term_rows, block_ids, num_segments=BOXES)

    coeffs = lax.fori_loop(0, SOURCES // block_rows, add_block, jnp.zeros((BOXES, 2 * points_sq), jnp.float32))
    devices = N_WIDE * N_NARROW
    coeffs = coeffs.reshape(devices, BOX_DEV, 2 * points_sq)
    kron_zero = interp_kron(Q, 0.0)
    kron_one = interp_kron(Q, 1.0)
    dev_ids = jnp.arange(devices, dtype=jnp.int32)
    masks = (1, 2, N_NARROW, 2 * N_NARROW, N_NARROW * N_WIDE // 2)
    for level_no, mask_bits in enumerate(masks):
        angle_rows = phase_table[level_no].reshape(devices, BOX_DEV, points_sq)
        rotated = rotate(coeffs, angle_rows)
        partner = rotated[jnp.bitwise_xor(dev_ids, mask_bits)]
        side_bit = (jnp.bitwise_and(dev_ids, mask_bits) != 0)[:, None, None]
        own_term = jnp.where(side_bit, apply_kron(rotated, kron_one), apply_kron(rotated, kron_zero))
        pair_term = jnp.where(side_bit, apply_kron(partner, kron_zero), apply_kron(partner, kron_one))
        coeffs = SQRT_HALF * (own_term + pair_term)
    return coeffs.reshape(BOXES, 2 * points_sq)
```

```python
import functools
import math

import jax
import jax.numpy as jnp
import numpy as np
from jax import lax
from jax.experimental import pallas as pl
from jax.experimental.pallas import tpu as pltpu
from jax.sharding import PartitionSpec as P

Q = 16


LEAF_GAIN = 5.0
SQRT_HALF = 0.7071067811865476
HIGH = lax.Precision.HIGHEST
MESH = pl.DeviceIdType.MESH
DEVICES = 128
RANKS = 128
FIELDS = 5
LEVELS = 5
SOURCES = 8192
LANES = 128
POINTS = 256
PARTS = 11
STEP = 8
GROUP = 8
GROUPS = DEVICES // GROUP
ROW_BITS = ((0, 6), (1, 5), (3, 4), (4, 3), (6, 2), (2, 1), (5, 0))
STEP_BITS = ((6, 6), (5, 2), (4, 0), (3, 5), (2, 1), (1, 4), (0, 3))
BF = jnp.bfloat16
F32 = jnp.float32


def partner_2(value, axis, apart):
    return lax.ppermute(value, axis, [(i, i ^ 1 << apart) for i in range(lax.axis_size(axis))])


def cheb_nodes(grid_order):
    counter = jnp.arange(grid_order, dtype=jnp.float32)
    return jnp.cos((2.0 * counter + 1.0) * math.pi / (2.0 * grid_order))


def lagrange(points, grid_order):
    node_list = cheb_nodes(grid_order)
    offsets = points[..., None] - node_list
    unit_col = jnp.ones_like(offsets[..., :1])
    before = jnp.cumprod(jnp.concatenate([unit_col, offsets[..., :-1]], -1), -1)
    after_prod = jnp.flip(
        jnp.cumprod(jnp.concatenate([unit_col, jnp.flip(offsets[..., 1:], -1)], -1), -1), -1
    )
    node_gaps = node_list[:, None] - node_list[None, :] + jnp.eye(grid_order, dtype=jnp.float32)
    node_prod = jnp.prod(node_gaps, 1)
    return before * after_prod / node_prod


def interp_kron(grid_order, side_value):
    node_list = cheb_nodes(grid_order)
    interp = lagrange((node_list + (2.0 * side_value - 1.0)) * 0.5, grid_order)
    return (interp[:, None, :, None] * interp[None, :, None, :]).reshape(
        grid_order * grid_order, grid_order * grid_order
    )


def apply_kron(coeffs, kron_matrix):
    flat_rows = coeffs.reshape(-1, kron_matrix.shape[0])
    result = lax.dot_general(
        flat_rows,
        kron_matrix,
        (((1,), (1,)), ((), ())),
        precision=HIGH,
        preferred_element_type=jnp.float32,
    )
    return result.reshape(coeffs.shape)


def rotate(coeffs, angle_rows):
    half_width = angle_rows.shape[-1]
    real_part = coeffs[..., :half_width]
    imag_part = coeffs[..., half_width:]
    cosine = jnp.cos(angle_rows)
    sine_val = jnp.sin(angle_rows)
    return jnp.concatenate(
        [cosine * real_part - sine_val * imag_part, sine_val * real_part + cosine * imag_part], -1
    )


def leaf_terms(first_pos, second_pos, phase_angle, weight, grid_order):
    first_basis = lagrange(first_pos, grid_order)
    second_basis = lagrange(second_pos, grid_order)
    outer_prod = (first_basis[:, :, None] * second_basis[:, None, :]).reshape(
        -1, grid_order * grid_order
    ) * (LEAF_GAIN * weight)[:, None]
    return jnp.concatenate(
        [outer_prod * jnp.cos(phase_angle)[:, None], outer_prod * jnp.sin(phase_angle)[:, None]], 1
    )


def combine(own_coeffs, pair_coeffs, side_bit, kron_zero, kron_one):
    kron_own = jnp.where(side_bit == 1, kron_one, kron_zero)
    kron_pair = jnp.where(side_bit == 1, kron_zero, kron_one)
    return SQRT_HALF * (apply_kron(own_coeffs, kron_own) + apply_kron(pair_coeffs, kron_pair))


def plain(positions, angles, weights, owner_dev, leaf_slot, phase_table):
    grid_order = Q
    points_sq = grid_order * grid_order
    wide_count = lax.axis_size("wide")
    narrow_count = lax.axis_size("narrow")
    devices = wide_count * narrow_count
    source_count = angles.shape[0]
    capacity = 4 * source_count // devices
    slot_count = devices * capacity
    box_count = phase_table.shape[1]
    target_dev = owner_dev[:, 0]
    dev_tags = jnp.arange(devices, dtype=jnp.int32)
    dev_counts = jnp.sum((target_dev[:, None] == dev_tags[None, :]).astype(jnp.int32), 0)
    dev_starts = jnp.cumsum(dev_counts) - dev_counts
    source_order = jnp.argsort(target_dev, stable=True)
    rank_grid = jnp.arange(capacity, dtype=jnp.int32)[None, :]
    slot_valid = (rank_grid < dev_counts[:, None]).reshape(slot_count)
    slot_pick = jnp.minimum(dev_starts[:, None] + rank_grid, source_count - 1).reshape(slot_count)
    slot_source = jnp.take(source_order, slot_pick, axis=0)
    records = jnp.stack([positions[0], positions[1], angles, weights])
    float_send = jnp.where(slot_valid[None, :], jnp.take(records, slot_source, axis=1), 0.0)
    index_send = jnp.where(slot_valid, jnp.take(leaf_slot, slot_source, axis=0), 0)[None, :]
    float_recv, index_recv = (
        lax.all_to_all(float_send, ("wide", "narrow"), split_axis=1, concat_axis=1, tiled=True),
        lax.all_to_all(index_send, ("wide", "narrow"), split_axis=1, concat_axis=1, tiled=True),
    )
    block_rows = math.gcd(slot_count, 2048)
    box_tags = jnp.arange(box_count, dtype=jnp.int32)

    def add_block(block_no, running):
        start = block_no * block_rows
        block_recs = lax.dynamic_slice_in_dim(float_recv, start, block_rows, 1)
        block_ids = lax.dynamic_slice_in_dim(index_recv[0], start, block_rows, 0)
        term_rows = leaf_terms(
            block_recs[0], block_recs[1], block_recs[2], block_recs[3], grid_order
        )
        one_hot = (block_ids[:, None] == box_tags[None, :]).astype(jnp.float32)
        return running + lax.dot_general(
            one_hot,
            term_rows,
            (((0,), (0,)), ((), ())),
            precision=HIGH,
            preferred_element_type=jnp.float32,
        )

    coeffs = lax.fori_loop(
        0, slot_count // block_rows, add_block, jnp.zeros((box_count, 2 * points_sq), jnp.float32)
    )
    kron_zero = interp_kron(grid_order, 0.0)
    kron_one = interp_kron(grid_order, 1.0)
    narrow_index = lax.axis_index("narrow")
    wide_index = lax.axis_index("wide")
    for bit_index in (0, 1):
        side_bit = jnp.bitwise_and(jnp.right_shift(narrow_index, bit_index), 1)
        rotated = rotate(coeffs, phase_table[bit_index])
        partner = partner_2(rotated, "narrow", bit_index)
        coeffs = combine(rotated, partner, side_bit, kron_zero, kron_one)
    top_bit = wide_count.bit_length() - 2
    for level_no, bit_index in ((2, 0), (3, 1), (4, top_bit)):
        side_bit = jnp.bitwise_and(jnp.right_shift(wide_index, bit_index), 1)
        rotated = rotate(coeffs, phase_table[level_no])
        partner = partner_2(rotated, "wide", bit_index)
        coeffs = combine(rotated, partner, side_bit, kron_zero, kron_one)
    return coeffs


NODES = np.cos((2 * np.arange(Q) + 1) * np.pi / (2 * Q))
GAPS = np.prod(NODES[:, None] - NODES[None, :] + np.eye(Q), 1)


def kron_table():
    blocks = []
    for side in (0.0, 1.0):
        points = (NODES + 2.0 * side - 1.0) * 0.5
        offsets = points[:, None] - NODES
        basis = np.stack(
            [np.prod(np.delete(offsets, k, 1), 1) / GAPS[k] for k in range(Q)], 1
        )
        blocks.append(np.kron(basis, basis).T)
    table = np.concatenate(blocks, 0) * SQRT_HALF
    high = table.astype(np.float32).astype(BF)
    low = (table - high.astype(np.float64)).astype(np.float32).astype(BF)
    return high, low


def series(function, degree):
    fit = np.polynomial.chebyshev.Chebyshev.interpolate(
        lambda t: function(np.sqrt(t)), degree, domain=[0.0, np.pi**2]
    )
    return [float(c) for c in fit.convert(kind=np.polynomial.Polynomial).coef]


COS_SERIES = series(np.cos, 7)
SIN_SERIES = series(lambda x: np.sinc(x / np.pi), 7)


def cos_sin(angle):
    square = angle * angle
    cosine = jnp.full_like(angle, COS_SERIES[-1])
    for c in COS_SERIES[-2::-1]:
        cosine = cosine * square + c
    sine = jnp.full_like(angle, SIN_SERIES[-1])
    for c in SIN_SERIES[-2::-1]:
        sine = sine * square + c
    return cosine, sine * angle


def basis_rows(points):
    offsets = [points - float(t) for t in NODES]
    before = [None, offsets[0]]
    for k in range(1, Q - 1):
        before.append(before[-1] * offsets[k])
    after = [None, offsets[Q - 1]]
    for k in range(Q - 2, 0, -1):
        after.append(after[-1] * offsets[k])
    after = after[::-1]
    rows = []
    for k in range(Q):
        scale = float(1.0 / GAPS[k])
        if k == 0:
            rows.append(after[0] * scale)
        elif k == Q - 1:
            rows.append(before[k] * scale)
        else:
            rows.append(before[k] * after[k] * scale)
    return rows


def split(value, count):
    parts = []
    for _ in range(count - 1):
        part = value.astype(BF).astype(F32)
        parts.append(part)
        value = value - part
    return parts + [value]


def move_bits(value, table):
    out = None
    for source, target in table:
        bit = lax.shift_left(
            lax.bitwise_and(lax.shift_right_logical(value, jnp.int32(source)), jnp.int32(1)),
            jnp.int32(target),
        )
        out = bit if out is None else lax.bitwise_or(out, bit)
    return out


def dot_nt(left, right):
    return lax.dot_general(left, right, (((1,), (1,)), ((), ())), preferred_element_type=F32)


def dot_nn(left, right):
    return jnp.dot(left, right, preferred_element_type=F32)


def body(
    pos, ang, wgt, own, slot, phase, high_k, low_k,
    out, flag,
    pair_s, box_s, wc_s, ws_s, left_s, right_s, packed_s,
    send_rec, recv_rec, send_ph, recv_ph, send_out,
    basis_v, basis_c, basis_s, terms_s, hot_s, leaf_s, state_s,
    rec_send, rec_recv, ph_send, ph_recv, out_send, out_recv, own_sem,
):
    me = lax.axis_index("wide") * 8 + lax.axis_index("narrow")
    my_row = move_bits(me, ROW_BITS)

    def device(t):
        return {"wide": lax.shift_right_logical(t, 3), "narrow": lax.bitwise_and(t, 7)}

    def partner_at(step):
        return lax.bitwise_xor(me, move_bits(step, STEP_BITS))

    barrier = pltpu.get_barrier_semaphore()

    def greet(step, carry):
        pl.semaphore_signal(
            barrier, inc=1, device_id=device(partner_at(step)), device_id_type=MESH
        )
        return carry

    lax.fori_loop(1, DEVICES, greet, 0)

    for level in range(LEVELS):
        for k in range(2):
            send_ph[level, pl.ds(k, 256, stride=2), :] = phase[level, :, k * LANES : (k + 1) * LANES]

    slots = slot[...]
    pair_s[...] = lax.shift_right_logical(slots, 1)
    box_s[...] = (
        move_bits(own[...], ROW_BITS) * 2 + lax.bitwise_and(slots, 1)
    ).astype(F32)
    cosine, sine = cos_sin(ang[...])
    gain = wgt[...] * LEAF_GAIN
    wc_s[...] = gain * cosine
    ws_s[...] = gain * sine
    packed_s[...] = jnp.zeros_like(packed_s)

    row_128 = lax.broadcasted_iota(jnp.int32, (128, LANES), 0)
    row_64 = lax.broadcasted_iota(jnp.int32, (64, LANES), 0)
    row_256f = lax.broadcasted_iota(jnp.int32, (256, LANES), 0).astype(F32)
    before = lax.broadcasted_iota(jnp.int32, (LANES, 256), 0)
    column = lax.broadcasted_iota(jnp.int32, (LANES, 256), 1)
    counter = jnp.where((before < column) | (column >= LANES), 1.0, 0.0).astype(BF)

    def pack(block, counts):
        for j in range(STEP):
            c = block * STEP + j
            lanes = slice(j * LANES, (j + 1) * LANES)
            pair = pair_s[pl.ds(c, 1), :]
            named = row_128 == pair
            seen = dot_nn(jnp.where(named, 1.0, 0.0).astype(BF), counter)
            rank = jnp.sum(
                jnp.where(named, seen[:, :LANES] + counts, 0.0), axis=0, keepdims=True
            )
            counts = counts + seen[:, LANES:]
            high_pair = lax.shift_right_logical(pair, 6).astype(F32) * RANKS
            place = jnp.where(rank < RANKS, high_pair + rank, -1.0)
            right_s[:, lanes] = jnp.where(row_256f == place, 1.0, 0.0).astype(BF)
            low_pair = row_64 == lax.bitwise_and(pair, 63)
            start = pl.multiple_of(c * LANES, LANES)
            values = (
                split(pos[0:1, pl.ds(start, LANES)], 3)
                + split(pos[1:2, pl.ds(start, LANES)], 3)
                + split(wc_s[pl.ds(c, 1), :], 2)
                + split(ws_s[pl.ds(c, 1), :], 2)
                + [box_s[pl.ds(c, 1), :]]
            )
            for p, value in enumerate(values):
                left_s[p * 64 : (p + 1) * 64, lanes] = jnp.where(low_pair, value, 0.0).astype(BF)
        packed_s[...] += dot_nt(left_s[...], right_s[...])
        return counts

    counts = lax.fori_loop(0, SOURCES // (STEP * LANES), pack, jnp.zeros((128, LANES), F32))
    too_many = jnp.max(jnp.max(counts, axis=0, keepdims=True), axis=1, keepdims=True)
    part = 0
    for field, count in enumerate((3, 3, 2, 2, 1)):
        value = packed_s[part * 64 : (part + 1) * 64, :]
        for extra in range(1, count):
            value = value + packed_s[(part + extra) * 64 : (part + extra + 1) * 64, :]
        if field == 0:
            value = jnp.where(too_many > RANKS, 4.0, value)
        part += count
        for half in range(2):
            send_rec[pl.ds(half * 512 + field, 64, stride=8), :] = value[
                :, half * LANES : (half + 1) * LANES
            ]

    pl.semaphore_wait(barrier, DEVICES - 1)

    own_rec = pltpu.make_async_copy(
        send_rec.at[pl.ds(pl.multiple_of(me * 8, 8), FIELDS)],
        recv_rec.at[pl.ds(0, FIELDS)],
        own_sem.at[0],
    )
    own_rec.start()
    own_ph = pltpu.make_async_copy(
        send_ph.at[:, pl.ds(pl.multiple_of(me * 4, 4), 4)],
        recv_ph.at[:, pl.ds(pl.multiple_of(my_row * 4, 4), 4)],
        own_sem.at[1],
    )
    own_ph.start()

    def send_records(step, carry):
        t = partner_at(step)
        pltpu.make_async_remote_copy(
            src_ref=send_rec.at[pl.ds(pl.multiple_of(t * 8, 8), FIELDS)],
            dst_ref=recv_rec.at[pl.ds(pl.multiple_of(step * 8, 8), FIELDS)],
            send_sem=rec_send,
            recv_sem=rec_recv.at[step // GROUP],
            device_id=device(t),
            device_id_type=MESH,
        ).start()
        return carry

    lax.fori_loop(1, DEVICES, send_records, 0)

    for level in range(LEVELS):

        def send_phases(step, carry):
            t = partner_at(step)
            pltpu.make_async_remote_copy(
                src_ref=send_ph.at[level, pl.ds(pl.multiple_of(t * 4, 4), 4)],
                dst_ref=recv_ph.at[level, pl.ds(pl.multiple_of(my_row * 4, 4), 4)],
                send_sem=ph_send,
                recv_sem=ph_recv.at[level],
                device_id=device(t),
                device_id_type=MESH,
            ).start()
            return carry

        lax.fori_loop(1, DEVICES, send_phases, 0)

    def wait_for(ref, rows, sem):
        view = ref.at[pl.ds(0, rows)]
        pltpu.make_async_copy(view, view, sem).wait()

    leaf_s[...] = jnp.zeros_like(leaf_s)
    own_rec.wait()

    def add_group(group, rows, largest):
        wait_for(recv_rec, rows, rec_recv.at[group])
        first = group * (GROUP * 8)
        if not isinstance(first, int):
            first = pl.multiple_of(first, GROUP * 8)
        field = [recv_rec[pl.ds(first + f, GROUP, stride=8), :] for f in range(FIELDS)]
        for k, value in enumerate(basis_rows(field[1])):
            basis_v[k * GROUP : (k + 1) * GROUP, :] = value
        for k, value in enumerate(basis_rows(field[0])):
            basis_c[k * GROUP : (k + 1) * GROUP, :] = value * field[2]
            basis_s[k * GROUP : (k + 1) * GROUP, :] = value * field[3]
        for s in range(GROUP):
            lanes = slice(s * LANES, (s + 1) * LANES)
            after = slice((GROUP + s) * LANES, (GROUP + s + 1) * LANES)
            second = basis_v[pl.ds(s, Q, stride=GROUP), :]
            for half, basis in enumerate((basis_c, basis_s)):
                for i in range(Q):
                    rows_i = slice(half * POINTS + i * Q, half * POINTS + (i + 1) * Q)
                    term = basis[i * GROUP + s : i * GROUP + s + 1, :] * second
                    high = term.astype(BF)
                    terms_s[rows_i, lanes] = high
                    terms_s[rows_i, after] = (term - high.astype(F32)).astype(BF)
            hot_s[:, lanes] = jnp.where(row_256f == field[4][s : s + 1, :], 1.0, 0.0).astype(BF)
        width = GROUP * LANES
        leaf_s[...] += dot_nt(terms_s[:, :width], hot_s[...]) + dot_nt(
            terms_s[:, width:], hot_s[...]
        )
        return jnp.maximum(largest, field[0])

    largest = add_group(0, (GROUP - 1) * FIELDS, jnp.zeros((GROUP, LANES), F32))
    largest = lax.fori_loop(
        1, GROUPS, lambda group, seen: add_group(group, GROUP * FIELDS, seen), largest
    )
    flag[...] = largest
    state_s[...] = leaf_s[...].T

    own_ph.wait()
    for level in range(LEVELS):
        wait_for(recv_ph.at[level], (DEVICES - 1) * 4, ph_recv.at[level])
        angle = jnp.concatenate(
            [recv_ph[level, pl.ds(k, 256, stride=2), :] for k in range(2)], axis=1
        )
        cosine, sine = cos_sin(angle)
        real, imag = state_s[:, :POINTS], state_s[:, POINTS:]
        apart = 128 >> level
        shape = (128 // apart, 2, apart, POINTS)
        turned = [
            (cosine * real - sine * imag).reshape(shape),
            (sine * real + cosine * imag).reshape(shape),
        ]
        sides = [
            jnp.concatenate([t[:, c].reshape(128, POINTS) for t in turned], axis=0)
            for c in range(2)
        ]
        both = jnp.concatenate(sides, axis=1)
        high = both.astype(BF)
        low = (both - high.astype(F32)).astype(BF)
        new = dot_nn(high, high_k[...]) + dot_nn(low, high_k[...]) + dot_nn(high, low_k[...])
        for half in range(2):
            part_new = new[half * 128 : (half + 1) * 128].reshape(128 // apart, 1, apart, POINTS)
            state_s[:, half * POINTS : (half + 1) * POINTS] = jnp.broadcast_to(
                part_new, shape
            ).reshape(256, POINTS)

    for k in range(4):
        send_out[pl.ds(k, 256, stride=4), :] = state_s[:, k * LANES : (k + 1) * LANES]
    own_out = pltpu.make_async_copy(
        send_out.at[pl.ds(pl.multiple_of(my_row * 8, 8), 8)],
        out.at[pl.ds(pl.multiple_of(me * 8, 8), 8)],
        own_sem.at[2],
    )
    own_out.start()

    def send_results(step, carry):
        t = partner_at(step)
        pltpu.make_async_remote_copy(
            src_ref=send_out.at[pl.ds(pl.multiple_of(move_bits(t, ROW_BITS) * 8, 8), 8)],
            dst_ref=out.at[pl.ds(pl.multiple_of(me * 8, 8), 8)],
            send_sem=out_send,
            recv_sem=out_recv,
            device_id=device(t),
            device_id_type=MESH,
        ).start()
        return carry

    lax.fori_loop(1, DEVICES, send_results, 0)
    own_out.wait()
    wait_for(out, (DEVICES - 1) * 8, out_recv)
    wait_for(send_rec, (DEVICES - 1) * FIELDS, rec_send)
    for level in range(LEVELS):
        wait_for(send_ph.at[level], (DEVICES - 1) * 4, ph_send)
    wait_for(send_out, (DEVICES - 1) * 8, out_send)


def fast(positions, angles, weights, owner_dev, leaf_slot, phase_table):
    high_k, low_k = kron_table()
    vmem = pl.BlockSpec(memory_space=pltpu.VMEM)
    dma = pltpu.SemaphoreType.DMA
    return pl.pallas_call(
        body,
        out_shape=(
            jax.ShapeDtypeStruct((1024, LANES), F32),
            jax.ShapeDtypeStruct((GROUP, LANES), F32),
        ),
        in_specs=[vmem] * 8,
        out_specs=(vmem, vmem),
        scratch_shapes=[
            pltpu.VMEM((64, LANES), jnp.int32),
            pltpu.VMEM((64, LANES), F32),
            pltpu.VMEM((64, LANES), F32),
            pltpu.VMEM((64, LANES), F32),
            pltpu.VMEM((PARTS * 64, STEP * LANES), BF),
            pltpu.VMEM((256, STEP * LANES), BF),
            pltpu.VMEM((PARTS * 64, 256), F32),
            pltpu.VMEM((1024, LANES), F32),
            pltpu.VMEM((1024, LANES), F32),
            pltpu.VMEM((LEVELS, 512, LANES), F32),
            pltpu.VMEM((LEVELS, 512, LANES), F32),
            pltpu.VMEM((1024, LANES), F32),
            pltpu.VMEM((Q * GROUP, LANES), F32),
            pltpu.VMEM((Q * GROUP, LANES), F32),
            pltpu.VMEM((Q * GROUP, LANES), F32),
            pltpu.VMEM((512, 2 * GROUP * LANES), BF),
            pltpu.VMEM((256, GROUP * LANES), BF),
            pltpu.VMEM((512, 256), F32),
            pltpu.VMEM((256, 512), F32),
            dma,
            dma((GROUPS,)),
            dma,
            dma((LEVELS,)),
            dma,
            dma,
            dma((3,)),
        ],
        compiler_params=pltpu.CompilerParams(
            collective_id=0, has_side_effects=True, vmem_limit_bytes=48 << 20
        ),
    )(
        positions,
        angles.reshape(64, LANES),
        weights.reshape(64, LANES),
        owner_dev.reshape(64, LANES),
        leaf_slot.reshape(64, LANES),
        phase_table,
        jnp.asarray(high_k),
        jnp.asarray(low_k),
    )


def shards(*arrays):
    result, largest = fast(*arrays)
    return lax.cond(
        jnp.max(largest) > 2.0, plain, lambda *_: result.reshape(256, 512), *arrays
    )


def solution(mesh):
    placed = (
        P(None, ("wide", "narrow")),
        P(("wide", "narrow")),
        P(("wide", "narrow")),
        P(("wide", "narrow"), None),
        P(("wide", "narrow")),
        P(None, ("wide", "narrow"), None),
    )
    return jax.shard_map(
        shards, mesh=mesh, in_specs=placed, out_specs=P(("wide", "narrow"), None), check_vma=False
    )
```

```python
import functools
import math

import jax
import jax.numpy as jnp
import numpy as np
from jax import lax
from jax.experimental import pallas as pl
from jax.experimental.pallas import tpu as pltpu
from jax.sharding import PartitionSpec as P

Q = 16


LEAF_GAIN = 5.0
SQRT_HALF = 0.7071067811865476
HIGH = lax.Precision.HIGHEST
MESH = pl.DeviceIdType.MESH
DEVICES = 128
RANKS = 128
FIELDS = 5
LEVELS = 5
SOURCES = 8192
LANES = 128
POINTS = 256
PARTS = 11
STEP = 8
GROUP = 8
GROUPS = DEVICES // GROUP
ROW_BITS = ((0, 6), (1, 5), (3, 4), (4, 3), (6, 2), (2, 1), (5, 0))
STEP_BITS = ((6, 6), (5, 2), (4, 0), (3, 5), (2, 1), (1, 4), (0, 3))
BF = jnp.bfloat16
F32 = jnp.float32


def partner_2(value, axis, apart):
    return lax.ppermute(value, axis, [(i, i ^ 1 << apart) for i in range(lax.axis_size(axis))])


def cheb_nodes(grid_order):
    counter = jnp.arange(grid_order, dtype=jnp.float32)
    return jnp.cos((2.0 * counter + 1.0) * math.pi / (2.0 * grid_order))


def lagrange(points, grid_order):
    node_list = cheb_nodes(grid_order)
    offsets = points[..., None] - node_list
    unit_col = jnp.ones_like(offsets[..., :1])
    before = jnp.cumprod(jnp.concatenate([unit_col, offsets[..., :-1]], -1), -1)
    after_prod = jnp.flip(
        jnp.cumprod(jnp.concatenate([unit_col, jnp.flip(offsets[..., 1:], -1)], -1), -1), -1
    )
    node_gaps = node_list[:, None] - node_list[None, :] + jnp.eye(grid_order, dtype=jnp.float32)
    node_prod = jnp.prod(node_gaps, 1)
    return before * after_prod / node_prod


def interp_kron(grid_order, side_value):
    node_list = cheb_nodes(grid_order)
    interp = lagrange((node_list + (2.0 * side_value - 1.0)) * 0.5, grid_order)
    return (interp[:, None, :, None] * interp[None, :, None, :]).reshape(
        grid_order * grid_order, grid_order * grid_order
    )


def apply_kron(coeffs, kron_matrix):
    flat_rows = coeffs.reshape(-1, kron_matrix.shape[0])
    result = lax.dot_general(
        flat_rows,
        kron_matrix,
        (((1,), (1,)), ((), ())),
        precision=HIGH,
        preferred_element_type=jnp.float32,
    )
    return result.reshape(coeffs.shape)


def rotate(coeffs, angle_rows):
    half_width = angle_rows.shape[-1]
    real_part = coeffs[..., :half_width]
    imag_part = coeffs[..., half_width:]
    cosine = jnp.cos(angle_rows)
    sine_val = jnp.sin(angle_rows)
    return jnp.concatenate(
        [cosine * real_part - sine_val * imag_part, sine_val * real_part + cosine * imag_part], -1
    )


def leaf_terms(first_pos, second_pos, phase_angle, weight, grid_order):
    first_basis = lagrange(first_pos, grid_order)
    second_basis = lagrange(second_pos, grid_order)
    outer_prod = (first_basis[:, :, None] * second_basis[:, None, :]).reshape(
        -1, grid_order * grid_order
    ) * (LEAF_GAIN * weight)[:, None]
    return jnp.concatenate(
        [outer_prod * jnp.cos(phase_angle)[:, None], outer_prod * jnp.sin(phase_angle)[:, None]], 1
    )


def combine(own_coeffs, pair_coeffs, side_bit, kron_zero, kron_one):
    kron_own = jnp.where(side_bit == 1, kron_one, kron_zero)
    kron_pair = jnp.where(side_bit == 1, kron_zero, kron_one)
    return SQRT_HALF * (apply_kron(own_coeffs, kron_own) + apply_kron(pair_coeffs, kron_pair))


def plain(positions, angles, weights, owner_dev, leaf_slot, phase_table):
    grid_order = Q
    points_sq = grid_order * grid_order
    wide_count = lax.axis_size("wide")
    narrow_count = lax.axis_size("narrow")
    devices = wide_count * narrow_count
    source_count = angles.shape[0]
    capacity = 4 * source_count // devices
    slot_count = devices * capacity
    box_count = phase_table.shape[1]
    target_dev = owner_dev[:, 0]
    dev_tags = jnp.arange(devices, dtype=jnp.int32)
    dev_counts = jnp.sum((target_dev[:, None] == dev_tags[None, :]).astype(jnp.int32), 0)
    dev_starts = jnp.cumsum(dev_counts) - dev_counts
    source_order = jnp.argsort(target_dev, stable=True)
    rank_grid = jnp.arange(capacity, dtype=jnp.int32)[None, :]
    slot_valid = (rank_grid < dev_counts[:, None]).reshape(slot_count)
    slot_pick = jnp.minimum(dev_starts[:, None] + rank_grid, source_count - 1).reshape(slot_count)
    slot_source = jnp.take(source_order, slot_pick, axis=0)
    records = jnp.stack([positions[0], positions[1], angles, weights])
    float_send = jnp.where(slot_valid[None, :], jnp.take(records, slot_source, axis=1), 0.0)
    index_send = jnp.where(slot_valid, jnp.take(leaf_slot, slot_source, axis=0), 0)[None, :]
    float_recv, index_recv = (
        lax.all_to_all(float_send, ("wide", "narrow"), split_axis=1, concat_axis=1, tiled=True),
        lax.all_to_all(index_send, ("wide", "narrow"), split_axis=1, concat_axis=1, tiled=True),
    )
    block_rows = math.gcd(slot_count, 2048)
    box_tags = jnp.arange(box_count, dtype=jnp.int32)

    def add_block(block_no, running):
        start = block_no * block_rows
        block_recs = lax.dynamic_slice_in_dim(float_recv, start, block_rows, 1)
        block_ids = lax.dynamic_slice_in_dim(index_recv[0], start, block_rows, 0)
        term_rows = leaf_terms(
            block_recs[0], block_recs[1], block_recs[2], block_recs[3], grid_order
        )
        one_hot = (block_ids[:, None] == box_tags[None, :]).astype(jnp.float32)
        return running + lax.dot_general(
            one_hot,
            term_rows,
            (((0,), (0,)), ((), ())),
            precision=HIGH,
            preferred_element_type=jnp.float32,
        )

    coeffs = lax.fori_loop(
        0, slot_count // block_rows, add_block, jnp.zeros((box_count, 2 * points_sq), jnp.float32)
    )
    kron_zero = interp_kron(grid_order, 0.0)
    kron_one = interp_kron(grid_order, 1.0)
    narrow_index = lax.axis_index("narrow")
    wide_index = lax.axis_index("wide")
    for bit_index in (0, 1):
        side_bit = jnp.bitwise_and(jnp.right_shift(narrow_index, bit_index), 1)
        rotated = rotate(coeffs, phase_table[bit_index])
        partner = partner_2(rotated, "narrow", bit_index)
        coeffs = combine(rotated, partner, side_bit, kron_zero, kron_one)
    top_bit = wide_count.bit_length() - 2
    for level_no, bit_index in ((2, 0), (3, 1), (4, top_bit)):
        side_bit = jnp.bitwise_and(jnp.right_shift(wide_index, bit_index), 1)
        rotated = rotate(coeffs, phase_table[level_no])
        partner = partner_2(rotated, "wide", bit_index)
        coeffs = combine(rotated, partner, side_bit, kron_zero, kron_one)
    return coeffs


NODES = np.cos((2 * np.arange(Q) + 1) * np.pi / (2 * Q))
GAPS = np.prod(NODES[:, None] - NODES[None, :] + np.eye(Q), 1)


def kron_table():
    blocks = []
    for side in (0.0, 1.0):
        points = (NODES + 2.0 * side - 1.0) * 0.5
        offsets = points[:, None] - NODES
        basis = np.stack(
            [np.prod(np.delete(offsets, k, 1), 1) / GAPS[k] for k in range(Q)], 1
        )
        blocks.append(np.kron(basis, basis).T)
    table = np.concatenate(blocks, 0) * SQRT_HALF
    high = table.astype(np.float32).astype(BF)
    low = (table - high.astype(np.float64)).astype(np.float32).astype(BF)
    return high, low


def series(function, degree):
    fit = np.polynomial.chebyshev.Chebyshev.interpolate(
        lambda t: function(np.sqrt(t)), degree, domain=[0.0, np.pi**2]
    )
    return [float(c) for c in fit.convert(kind=np.polynomial.Polynomial).coef]


COS_SERIES = series(np.cos, 7)
SIN_SERIES = series(lambda x: np.sinc(x / np.pi), 7)


def cos_sin(angle):
    square = angle * angle
    cosine = jnp.full_like(angle, COS_SERIES[-1])
    for c in COS_SERIES[-2::-1]:
        cosine = cosine * square + c
    sine = jnp.full_like(angle, SIN_SERIES[-1])
    for c in SIN_SERIES[-2::-1]:
        sine = sine * square + c
    return cosine, sine * angle


def basis_rows(points):
    offsets = [points - float(t) for t in NODES]
    before = [None, offsets[0]]
    for k in range(1, Q - 1):
        before.append(before[-1] * offsets[k])
    after = [None, offsets[Q - 1]]
    for k in range(Q - 2, 0, -1):
        after.append(after[-1] * offsets[k])
    after = after[::-1]
    rows = []
    for k in range(Q):
        scale = float(1.0 / GAPS[k])
        if k == 0:
            rows.append(after[0] * scale)
        elif k == Q - 1:
            rows.append(before[k] * scale)
        else:
            rows.append(before[k] * after[k] * scale)
    return rows


def split(value, count):
    parts = []
    for _ in range(count - 1):
        part = value.astype(BF).astype(F32)
        parts.append(part)
        value = value - part
    return parts + [value]


def move_bits(value, table):
    out = None
    for source, target in table:
        bit = lax.shift_left(
            lax.bitwise_and(lax.shift_right_logical(value, jnp.int32(source)), jnp.int32(1)),
            jnp.int32(target),
        )
        out = bit if out is None else lax.bitwise_or(out, bit)
    return out


def move_bits_of(number, table):
    return sum(((number >> source) & 1) << target for source, target in table)


GROUP_BITS = tuple((step - 3, bit) for step, bit in STEP_BITS if step >= 3)
GROUP_ROW_BITS = tuple((step, dict(ROW_BITS)[bit]) for step, bit in GROUP_BITS)


def dot_nt(left, right):
    return lax.dot_general(left, right, (((1,), (1,)), ((), ())), preferred_element_type=F32)


def dot_nn(left, right):
    return jnp.dot(left, right, preferred_element_type=F32)


def body(
    pos_h, ang_h, wgt_h, own_h, slot_h, phase_h, high_h, low_h,
    out, flag,
    pos, ang, wgt, own, slot, phase, high_k, low_k, load_sem,
    pair_s, box_s, wc_s, ws_s, left_s, right_s, packed_s,
    send_rec, recv_rec, send_ph, recv_ph, send_out,
    basis_v, basis_c, basis_s, terms_a, terms_b, hot_a, hot_b, leaf_s, state_s,
    rec_send, rec_recv, ph_send, ph_recv, out_send, out_recv, own_sem,
):
    me = lax.axis_index("wide") * 8 + lax.axis_index("narrow")
    my_row = move_bits(me, ROW_BITS)

    def device(t):
        return {"wide": lax.shift_right_logical(t, 3), "narrow": lax.bitwise_and(t, 7)}

    def for_partners(act):
        def visit(group, first):
            base = me if first else lax.bitwise_xor(me, move_bits(group, GROUP_BITS))
            base_row = my_row if first else lax.bitwise_xor(my_row, move_bits(group, GROUP_ROW_BITS))
            for j in range(1 if first else 0, GROUP):
                offset = move_bits_of(j, STEP_BITS)
                act(
                    group,
                    j,
                    lax.bitwise_xor(base, offset),
                    lax.bitwise_xor(base_row, move_bits_of(offset, ROW_BITS)),
                )

        visit(0, True)

        def later(group, carry):
            visit(group, False)
            return carry

        lax.fori_loop(1, GROUPS, later, 0)

    loads = [
        pltpu.make_async_copy(source, target, load_sem.at[i])
        for i, (source, target) in enumerate(
            (
                (phase_h, phase),
                (pos_h, pos),
                (ang_h, ang),
                (wgt_h, wgt),
                (own_h, own),
                (slot_h, slot),
                (high_h, high_k),
                (low_h, low_k),
            )
        )
    ]
    for load in loads:
        load.start()

    barrier = pltpu.get_barrier_semaphore()

    def greet(group, j, t, row):
        pl.semaphore_signal(barrier, inc=1, device_id=device(t), device_id_type=MESH)

    for_partners(greet)

    def rows_of(block, count):
        first = block * 8
        return pl.ds(first if isinstance(first, int) else pl.multiple_of(first, 8), count)

    for load in loads[:6]:
        load.wait()

    for level in range(LEVELS):
        for k in range(2):
            send_ph[level, pl.ds(k, 256, stride=2), :] = phase[level, :, k * LANES : (k + 1) * LANES]

    slots = slot[...]
    pair_s[...] = lax.shift_right_logical(slots, 1)
    box_s[...] = (
        move_bits(own[...], ROW_BITS) * 2 + lax.bitwise_and(slots, 1)
    ).astype(F32)
    cosine, sine = cos_sin(ang[...])
    gain = wgt[...] * LEAF_GAIN
    wc_s[...] = gain * cosine
    ws_s[...] = gain * sine
    packed_s[...] = jnp.zeros_like(packed_s)

    row_128 = lax.broadcasted_iota(jnp.int32, (128, LANES), 0)
    row_64 = lax.broadcasted_iota(jnp.int32, (64, LANES), 0)
    row_256f = lax.broadcasted_iota(jnp.int32, (256, LANES), 0).astype(F32)
    before = lax.broadcasted_iota(jnp.int32, (LANES, 256), 0)
    column = lax.broadcasted_iota(jnp.int32, (LANES, 256), 1)
    counter = jnp.where((before < column) | (column >= LANES), 1.0, 0.0).astype(BF)

    def pack(block, counts):
        for j in range(STEP):
            c = block * STEP + j
            lanes = slice(j * LANES, (j + 1) * LANES)
            pair = pair_s[pl.ds(c, 1), :]
            named = row_128 == pair
            seen = dot_nn(jnp.where(named, 1.0, 0.0).astype(BF), counter)
            rank = jnp.sum(
                jnp.where(named, seen[:, :LANES] + counts, 0.0), axis=0, keepdims=True
            )
            counts = counts + seen[:, LANES:]
            high_pair = lax.shift_right_logical(pair, 6).astype(F32) * RANKS
            place = jnp.where(rank < RANKS, high_pair + rank, -1.0)
            right_s[:, lanes] = jnp.where(row_256f == place, 1.0, 0.0).astype(BF)
            low_pair = row_64 == lax.bitwise_and(pair, 63)
            start = pl.multiple_of(c * LANES, LANES)
            values = (
                split(pos[0:1, pl.ds(start, LANES)], 3)
                + split(pos[1:2, pl.ds(start, LANES)], 3)
                + split(wc_s[pl.ds(c, 1), :], 2)
                + split(ws_s[pl.ds(c, 1), :], 2)
                + [box_s[pl.ds(c, 1), :]]
            )
            for p, value in enumerate(values):
                left_s[p * 64 : (p + 1) * 64, lanes] = jnp.where(low_pair, value, 0.0).astype(BF)
        packed_s[...] += dot_nt(left_s[...], right_s[...])
        return counts

    counts = lax.fori_loop(0, SOURCES // (STEP * LANES), pack, jnp.zeros((128, LANES), F32))
    too_many = jnp.max(jnp.max(counts, axis=0, keepdims=True), axis=1, keepdims=True)
    part = 0
    for field, count in enumerate((3, 3, 2, 2, 1)):
        value = packed_s[part * 64 : (part + 1) * 64, :]
        for extra in range(1, count):
            value = value + packed_s[(part + extra) * 64 : (part + extra + 1) * 64, :]
        if field == 0:
            value = jnp.where(too_many > RANKS, 4.0, value)
        part += count
        for half in range(2):
            send_rec[pl.ds(half * 512 + field, 64, stride=8), :] = value[
                :, half * LANES : (half + 1) * LANES
            ]

    pl.semaphore_wait(barrier, DEVICES - 1)

    own_rec = pltpu.make_async_copy(
        send_rec.at[pl.ds(pl.multiple_of(me * 8, 8), FIELDS)],
        recv_rec.at[pl.ds(0, FIELDS)],
        own_sem.at[0],
    )
    own_rec.start()
    own_ph = pltpu.make_async_copy(
        send_ph.at[:, pl.ds(pl.multiple_of(me * 4, 4), 4)],
        recv_ph.at[:, pl.ds(pl.multiple_of(my_row * 4, 4), 4)],
        own_sem.at[1],
    )
    own_ph.start()

    def send_records(group, j, t, row):
        pltpu.make_async_remote_copy(
            src_ref=send_rec.at[pl.ds(pl.multiple_of(t * 8, 8), FIELDS)],
            dst_ref=recv_rec.at[rows_of(group * GROUP + j, FIELDS)],
            send_sem=rec_send,
            recv_sem=rec_recv.at[group],
            device_id=device(t),
            device_id_type=MESH,
        ).start()

    for_partners(send_records)

    for level in range(LEVELS):

        def send_phases(group, j, t, row):
            pltpu.make_async_remote_copy(
                src_ref=send_ph.at[level, pl.ds(pl.multiple_of(t * 4, 4), 4)],
                dst_ref=recv_ph.at[level, pl.ds(pl.multiple_of(my_row * 4, 4), 4)],
                send_sem=ph_send,
                recv_sem=ph_recv.at[level],
                device_id=device(t),
                device_id_type=MESH,
            ).start()

        for_partners(send_phases)

    def wait_for(ref, rows, sem):
        view = ref.at[pl.ds(0, rows)]
        pltpu.make_async_copy(view, view, sem).wait()

    leaf_s[...] = jnp.zeros_like(leaf_s)
    own_rec.wait()

    def arrived(group):
        wait_for(recv_rec, GROUP * FIELDS, rec_recv.at[group])

    def build(group, terms, hot, largest):
        first = group * (GROUP * 8)
        if not isinstance(first, int):
            first = pl.multiple_of(first, GROUP * 8)
        field = [recv_rec[pl.ds(first + f, GROUP, stride=8), :] for f in range(FIELDS)]
        for k, value in enumerate(basis_rows(field[1])):
            basis_v[k * GROUP : (k + 1) * GROUP, :] = value
        for k, value in enumerate(basis_rows(field[0])):
            basis_c[k * GROUP : (k + 1) * GROUP, :] = value * field[2]
            basis_s[k * GROUP : (k + 1) * GROUP, :] = value * field[3]
        for s in range(GROUP):
            lanes = slice(s * LANES, (s + 1) * LANES)
            after = slice((GROUP + s) * LANES, (GROUP + s + 1) * LANES)
            second = basis_v[pl.ds(s, Q, stride=GROUP), :]
            for half, basis in enumerate((basis_c, basis_s)):
                for i in range(Q):
                    rows_i = slice(half * POINTS + i * Q, half * POINTS + (i + 1) * Q)
                    term = basis[i * GROUP + s : i * GROUP + s + 1, :] * second
                    high = term.astype(BF)
                    terms[rows_i, lanes] = high
                    terms[rows_i, after] = (term - high.astype(F32)).astype(BF)
            named = jnp.where(row_256f == field[4][s : s + 1, :], 1.0, 0.0).astype(BF)
            hot[:, lanes] = named
            hot[:, after] = named
        return jnp.maximum(largest, field[0])

    def add(terms, hot):
        leaf_s[...] += dot_nt(terms[...], hot[...])

    wait_for(recv_rec, (GROUP - 1) * FIELDS, rec_recv.at[0])
    largest = build(0, terms_a, hot_a, jnp.zeros((GROUP, LANES), F32))

    def two_groups(pair, largest):
        arrived(2 * pair + 1)
        arrived(2 * pair + 2)
        largest = build(2 * pair + 1, terms_b, hot_b, largest)
        add(terms_a, hot_a)
        largest = build(2 * pair + 2, terms_a, hot_a, largest)
        add(terms_b, hot_b)
        return largest

    largest = lax.fori_loop(0, GROUPS // 2 - 1, two_groups, largest)
    arrived(GROUPS - 1)
    largest = build(GROUPS - 1, terms_b, hot_b, largest)
    add(terms_a, hot_a)
    add(terms_b, hot_b)
    flag[0, 0] = jnp.max(largest)
    for load in loads[6:]:
        load.wait()
    state_s[...] = leaf_s[...].T

    own_ph.wait()
    for level in range(LEVELS):
        wait_for(recv_ph.at[level], (DEVICES - 1) * 4, ph_recv.at[level])
        angle = jnp.concatenate(
            [recv_ph[level, pl.ds(k, 256, stride=2), :] for k in range(2)], axis=1
        )
        cosine, sine = cos_sin(angle)
        real, imag = state_s[:, :POINTS], state_s[:, POINTS:]
        apart = 128 >> level
        shape = (128 // apart, 2, apart, POINTS)
        turned = [
            (cosine * real - sine * imag).reshape(shape),
            (sine * real + cosine * imag).reshape(shape),
        ]
        sides = [
            jnp.concatenate([t[:, c].reshape(128, POINTS) for t in turned], axis=0)
            for c in range(2)
        ]
        both = jnp.concatenate(sides, axis=1)
        high = both.astype(BF)
        low = (both - high.astype(F32)).astype(BF)
        new = dot_nn(high, high_k[...]) + dot_nn(low, high_k[...]) + dot_nn(high, low_k[...])
        for half in range(2):
            part_new = new[half * 128 : (half + 1) * 128].reshape(128 // apart, 1, apart, POINTS)
            state_s[:, half * POINTS : (half + 1) * POINTS] = jnp.broadcast_to(
                part_new, shape
            ).reshape(256, POINTS)

    for k in range(4):
        send_out[pl.ds(k, 256, stride=4), :] = state_s[:, k * LANES : (k + 1) * LANES]
    own_out = pltpu.make_async_copy(
        send_out.at[pl.ds(pl.multiple_of(my_row * 8, 8), 8)],
        out.at[pl.ds(pl.multiple_of(me * 8, 8), 8)],
        own_sem.at[2],
    )
    own_out.start()

    def send_results(group, j, t, row):
        pltpu.make_async_remote_copy(
            src_ref=send_out.at[rows_of(row, 8)],
            dst_ref=out.at[pl.ds(pl.multiple_of(me * 8, 8), 8)],
            send_sem=out_send,
            recv_sem=out_recv,
            device_id=device(t),
            device_id_type=MESH,
        ).start()

    for_partners(send_results)
    own_out.wait()
    wait_for(out, (DEVICES - 1) * 8, out_recv)
    wait_for(send_rec, (DEVICES - 1) * FIELDS, rec_send)
    for level in range(LEVELS):
        wait_for(send_ph.at[level], (DEVICES - 1) * 4, ph_send)
    wait_for(send_out, (DEVICES - 1) * 8, out_send)


def fast(positions, angles, weights, owner_dev, leaf_slot, phase_table):
    high_k, low_k = kron_table()
    dma = pltpu.SemaphoreType.DMA
    return pl.pallas_call(
        body,
        out_shape=(
            jax.ShapeDtypeStruct((1024, LANES), F32),
            jax.ShapeDtypeStruct((1, 1), F32),
        ),
        in_specs=[pl.BlockSpec(memory_space=pl.ANY)] * 8,
        out_specs=(
            pl.BlockSpec(memory_space=pl.ANY),
            pl.BlockSpec(memory_space=pltpu.SMEM),
        ),
        scratch_shapes=[
            pltpu.VMEM((2, SOURCES), F32),
            pltpu.VMEM((64, LANES), F32),
            pltpu.VMEM((64, LANES), F32),
            pltpu.VMEM((64, LANES), jnp.int32),
            pltpu.VMEM((64, LANES), jnp.int32),
            pltpu.VMEM((LEVELS, 256, POINTS), F32),
            pltpu.VMEM((512, POINTS), BF),
            pltpu.VMEM((512, POINTS), BF),
            dma((8,)),
            pltpu.VMEM((64, LANES), jnp.int32),
            pltpu.VMEM((64, LANES), F32),
            pltpu.VMEM((64, LANES), F32),
            pltpu.VMEM((64, LANES), F32),
            pltpu.VMEM((PARTS * 64, STEP * LANES), BF),
            pltpu.VMEM((256, STEP * LANES), BF),
            pltpu.VMEM((PARTS * 64, 256), F32),
            pltpu.VMEM((1024, LANES), F32),
            pltpu.VMEM((1024, LANES), F32),
            pltpu.VMEM((LEVELS, 512, LANES), F32),
            pltpu.VMEM((LEVELS, 512, LANES), F32),
            pltpu.VMEM((1024, LANES), F32),
            pltpu.VMEM((Q * GROUP, LANES), F32),
            pltpu.VMEM((Q * GROUP, LANES), F32),
            pltpu.VMEM((Q * GROUP, LANES), F32),
            pltpu.VMEM((512, 2 * GROUP * LANES), BF),
            pltpu.VMEM((512, 2 * GROUP * LANES), BF),
            pltpu.VMEM((256, 2 * GROUP * LANES), BF),
            pltpu.VMEM((256, 2 * GROUP * LANES), BF),
            pltpu.VMEM((512, 256), F32),
            pltpu.VMEM((256, 512), F32),
            dma,
            dma((GROUPS,)),
            dma,
            dma((LEVELS,)),
            dma,
            dma,
            dma((3,)),
        ],
        compiler_params=pltpu.CompilerParams(
            collective_id=0, has_side_effects=True, vmem_limit_bytes=56 << 20
        ),
    )(
        positions,
        angles.reshape(64, LANES),
        weights.reshape(64, LANES),
        owner_dev.reshape(64, LANES),
        leaf_slot.reshape(64, LANES),
        phase_table,
        jnp.asarray(high_k),
        jnp.asarray(low_k),
    )


def shards(*arrays):
    result, largest = fast(*arrays)
    return lax.cond(
        largest[0, 0] > 2.0, plain, lambda *_: result.reshape(256, 512), *arrays
    )


def solution(mesh):
    placed = (
        P(None, ("wide", "narrow")),
        P(("wide", "narrow")),
        P(("wide", "narrow")),
        P(("wide", "narrow"), None),
        P(("wide", "narrow")),
        P(None, ("wide", "narrow"), None),
    )
    return jax.shard_map(
        shards, mesh=mesh, in_specs=placed, out_specs=P(("wide", "narrow"), None), check_vma=False
    )
```

```python
import functools
import math

import jax
import jax.numpy as jnp
import numpy as np
from jax import lax
from jax.experimental import pallas as pl
from jax.experimental.pallas import tpu as pltpu
from jax.sharding import PartitionSpec as P

Q = 16


LEAF_GAIN = 5.0
SQRT_HALF = 0.7071067811865476
HIGH = lax.Precision.HIGHEST
MESH = pl.DeviceIdType.MESH
DEVICES = 128
RANKS = 128
FIELDS = 5
LEVELS = 5
SOURCES = 8192
LANES = 128
POINTS = 256
PARTS = 11
STEP = 8
GROUP = 8
GROUPS = DEVICES // GROUP
BLOCKS = SOURCES // (STEP * LANES)
EARLY = 3
BATCHES = (slice(0, 3), slice(3, 5))
ROW_BITS = ((0, 6), (1, 5), (3, 4), (4, 3), (6, 2), (2, 1), (5, 0))
STEP_BITS = ((6, 6), (5, 2), (4, 0), (3, 5), (2, 1), (1, 4), (0, 3))
BF = jnp.bfloat16
F32 = jnp.float32


def partner_2(value, axis, apart):
    return lax.ppermute(value, axis, [(i, i ^ 1 << apart) for i in range(lax.axis_size(axis))])


def cheb_nodes(grid_order):
    counter = jnp.arange(grid_order, dtype=jnp.float32)
    return jnp.cos((2.0 * counter + 1.0) * math.pi / (2.0 * grid_order))


def lagrange(points, grid_order):
    node_list = cheb_nodes(grid_order)
    offsets = points[..., None] - node_list
    unit_col = jnp.ones_like(offsets[..., :1])
    before = jnp.cumprod(jnp.concatenate([unit_col, offsets[..., :-1]], -1), -1)
    after_prod = jnp.flip(
        jnp.cumprod(jnp.concatenate([unit_col, jnp.flip(offsets[..., 1:], -1)], -1), -1), -1
    )
    node_gaps = node_list[:, None] - node_list[None, :] + jnp.eye(grid_order, dtype=jnp.float32)
    node_prod = jnp.prod(node_gaps, 1)
    return before * after_prod / node_prod


def interp_kron(grid_order, side_value):
    node_list = cheb_nodes(grid_order)
    interp = lagrange((node_list + (2.0 * side_value - 1.0)) * 0.5, grid_order)
    return (interp[:, None, :, None] * interp[None, :, None, :]).reshape(
        grid_order * grid_order, grid_order * grid_order
    )


def apply_kron(coeffs, kron_matrix):
    flat_rows = coeffs.reshape(-1, kron_matrix.shape[0])
    result = lax.dot_general(
        flat_rows,
        kron_matrix,
        (((1,), (1,)), ((), ())),
        precision=HIGH,
        preferred_element_type=jnp.float32,
    )
    return result.reshape(coeffs.shape)


def rotate(coeffs, angle_rows):
    half_width = angle_rows.shape[-1]
    real_part = coeffs[..., :half_width]
    imag_part = coeffs[..., half_width:]
    cosine = jnp.cos(angle_rows)
    sine_val = jnp.sin(angle_rows)
    return jnp.concatenate(
        [cosine * real_part - sine_val * imag_part, sine_val * real_part + cosine * imag_part], -1
    )


def leaf_terms(first_pos, second_pos, phase_angle, weight, grid_order):
    first_basis = lagrange(first_pos, grid_order)
    second_basis = lagrange(second_pos, grid_order)
    outer_prod = (first_basis[:, :, None] * second_basis[:, None, :]).reshape(
        -1, grid_order * grid_order
    ) * (LEAF_GAIN * weight)[:, None]
    return jnp.concatenate(
        [outer_prod * jnp.cos(phase_angle)[:, None], outer_prod * jnp.sin(phase_angle)[:, None]], 1
    )


def combine(own_coeffs, pair_coeffs, side_bit, kron_zero, kron_one):
    kron_own = jnp.where(side_bit == 1, kron_one, kron_zero)
    kron_pair = jnp.where(side_bit == 1, kron_zero, kron_one)
    return SQRT_HALF * (apply_kron(own_coeffs, kron_own) + apply_kron(pair_coeffs, kron_pair))


def plain(positions, angles, weights, owner_dev, leaf_slot, phase_table):
    grid_order = Q
    points_sq = grid_order * grid_order
    wide_count = lax.axis_size("wide")
    narrow_count = lax.axis_size("narrow")
    devices = wide_count * narrow_count
    source_count = angles.shape[0]
    capacity = 4 * source_count // devices
    slot_count = devices * capacity
    box_count = phase_table.shape[1]
    target_dev = owner_dev[:, 0]
    dev_tags = jnp.arange(devices, dtype=jnp.int32)
    dev_counts = jnp.sum((target_dev[:, None] == dev_tags[None, :]).astype(jnp.int32), 0)
    dev_starts = jnp.cumsum(dev_counts) - dev_counts
    source_order = jnp.argsort(target_dev, stable=True)
    rank_grid = jnp.arange(capacity, dtype=jnp.int32)[None, :]
    slot_valid = (rank_grid < dev_counts[:, None]).reshape(slot_count)
    slot_pick = jnp.minimum(dev_starts[:, None] + rank_grid, source_count - 1).reshape(slot_count)
    slot_source = jnp.take(source_order, slot_pick, axis=0)
    records = jnp.stack([positions[0], positions[1], angles, weights])
    float_send = jnp.where(slot_valid[None, :], jnp.take(records, slot_source, axis=1), 0.0)
    index_send = jnp.where(slot_valid, jnp.take(leaf_slot, slot_source, axis=0), 0)[None, :]
    float_recv, index_recv = (
        lax.all_to_all(float_send, ("wide", "narrow"), split_axis=1, concat_axis=1, tiled=True),
        lax.all_to_all(index_send, ("wide", "narrow"), split_axis=1, concat_axis=1, tiled=True),
    )
    block_rows = math.gcd(slot_count, 2048)
    box_tags = jnp.arange(box_count, dtype=jnp.int32)

    def add_block(block_no, running):
        start = block_no * block_rows
        block_recs = lax.dynamic_slice_in_dim(float_recv, start, block_rows, 1)
        block_ids = lax.dynamic_slice_in_dim(index_recv[0], start, block_rows, 0)
        term_rows = leaf_terms(
            block_recs[0], block_recs[1], block_recs[2], block_recs[3], grid_order
        )
        one_hot = (block_ids[:, None] == box_tags[None, :]).astype(jnp.float32)
        return running + lax.dot_general(
            one_hot,
            term_rows,
            (((0,), (0,)), ((), ())),
            precision=HIGH,
            preferred_element_type=jnp.float32,
        )

    coeffs = lax.fori_loop(
        0, slot_count // block_rows, add_block, jnp.zeros((box_count, 2 * points_sq), jnp.float32)
    )
    kron_zero = interp_kron(grid_order, 0.0)
    kron_one = interp_kron(grid_order, 1.0)
    narrow_index = lax.axis_index("narrow")
    wide_index = lax.axis_index("wide")
    for bit_index in (0, 1):
        side_bit = jnp.bitwise_and(jnp.right_shift(narrow_index, bit_index), 1)
        rotated = rotate(coeffs, phase_table[bit_index])
        partner = partner_2(rotated, "narrow", bit_index)
        coeffs = combine(rotated, partner, side_bit, kron_zero, kron_one)
    top_bit = wide_count.bit_length() - 2
    for level_no, bit_index in ((2, 0), (3, 1), (4, top_bit)):
        side_bit = jnp.bitwise_and(jnp.right_shift(wide_index, bit_index), 1)
        rotated = rotate(coeffs, phase_table[level_no])
        partner = partner_2(rotated, "wide", bit_index)
        coeffs = combine(rotated, partner, side_bit, kron_zero, kron_one)
    return coeffs


NODES = np.cos((2 * np.arange(Q) + 1) * np.pi / (2 * Q))
GAPS = np.prod(NODES[:, None] - NODES[None, :] + np.eye(Q), 1)


def kron_table():
    blocks = []
    for side in (0.0, 1.0):
        points = (NODES + 2.0 * side - 1.0) * 0.5
        offsets = points[:, None] - NODES
        basis = np.stack(
            [np.prod(np.delete(offsets, k, 1), 1) / GAPS[k] for k in range(Q)], 1
        )
        blocks.append(np.kron(basis, basis).T)
    table = np.concatenate(blocks, 0) * SQRT_HALF
    high = table.astype(np.float32).astype(BF)
    low = (table - high.astype(np.float64)).astype(np.float32).astype(BF)
    return high, low


def series(function, degree):
    fit = np.polynomial.chebyshev.Chebyshev.interpolate(
        lambda t: function(np.sqrt(t)), degree, domain=[0.0, np.pi**2]
    )
    return [float(c) for c in fit.convert(kind=np.polynomial.Polynomial).coef]


COS_SERIES = series(np.cos, 7)
SIN_SERIES = series(lambda x: np.sinc(x / np.pi), 7)


def cos_sin(angle):
    square = angle * angle
    cosine = jnp.full_like(angle, COS_SERIES[-1])
    for c in COS_SERIES[-2::-1]:
        cosine = cosine * square + c
    sine = jnp.full_like(angle, SIN_SERIES[-1])
    for c in SIN_SERIES[-2::-1]:
        sine = sine * square + c
    return cosine, sine * angle


def basis_rows(points):
    offsets = [points - float(t) for t in NODES]
    before = [None, offsets[0]]
    for k in range(1, Q - 1):
        before.append(before[-1] * offsets[k])
    after = [None, offsets[Q - 1]]
    for k in range(Q - 2, 0, -1):
        after.append(after[-1] * offsets[k])
    after = after[::-1]
    rows = []
    for k in range(Q):
        scale = float(1.0 / GAPS[k])
        if k == 0:
            rows.append(after[0] * scale)
        elif k == Q - 1:
            rows.append(before[k] * scale)
        else:
            rows.append(before[k] * after[k] * scale)
    return rows


def split(value, count):
    parts = []
    for _ in range(count - 1):
        part = value.astype(BF).astype(F32)
        parts.append(part)
        value = value - part
    return parts + [value]


def move_bits(value, table):
    out = None
    for source, target in table:
        bit = lax.shift_left(
            lax.bitwise_and(lax.shift_right_logical(value, jnp.int32(source)), jnp.int32(1)),
            jnp.int32(target),
        )
        out = bit if out is None else lax.bitwise_or(out, bit)
    return out


def move_bits_of(number, table):
    return sum(((number >> source) & 1) << target for source, target in table)


GROUP_BITS = tuple((step - 3, bit) for step, bit in STEP_BITS if step >= 3)
GROUP_ROW_BITS = tuple((step, dict(ROW_BITS)[bit]) for step, bit in GROUP_BITS)


def dot_nt(left, right):
    return lax.dot_general(left, right, (((1,), (1,)), ((), ())), preferred_element_type=F32)


def dot_nn(left, right):
    return jnp.dot(left, right, preferred_element_type=F32)


def body(
    pos_h, ang_h, wgt_h, own_h, slot_h, phase_h, high_h, low_h,
    out, flag,
    pos, ang, wgt, own, slot, phase, high_k, low_k, load_sem,
    pair_s, box_s, wc_s, ws_s, left_a, left_b, right_a, right_b, packed_s,
    send_rec, recv_rec, send_ph, recv_ph, send_out,
    basis_v, basis_c, basis_s, terms_s, hot_s, leaf_s, state_s, angle_s,
    rec_send, rec_recv, ph_send, ph_recv, out_send, out_recv, own_sem,
):
    me = lax.axis_index("wide") * 8 + lax.axis_index("narrow")
    my_row = move_bits(me, ROW_BITS)

    def device(t):
        return {"wide": lax.shift_right_logical(t, 3), "narrow": lax.bitwise_and(t, 7)}

    def for_partners(act):
        def visit(group, first):
            base = me if first else lax.bitwise_xor(me, move_bits(group, GROUP_BITS))
            base_row = my_row if first else lax.bitwise_xor(my_row, move_bits(group, GROUP_ROW_BITS))
            for j in range(1 if first else 0, GROUP):
                offset = move_bits_of(j, STEP_BITS)
                act(
                    group,
                    j,
                    lax.bitwise_xor(base, offset),
                    lax.bitwise_xor(base_row, move_bits_of(offset, ROW_BITS)),
                )

        visit(0, True)

        def later(group, carry):
            visit(group, False)
            return carry

        lax.fori_loop(1, GROUPS, later, 0)

    loads = [
        pltpu.make_async_copy(source, target, load_sem.at[i])
        for i, (source, target) in enumerate(
            (
                (phase_h, phase),
                (pos_h, pos),
                (ang_h, ang),
                (wgt_h, wgt),
                (own_h, own),
                (slot_h, slot),
                (high_h, high_k),
                (low_h, low_k),
            )
        )
    ]
    for load in loads:
        load.start()

    barrier = pltpu.get_barrier_semaphore()

    def greet(group, j, t, row):
        pl.semaphore_signal(barrier, inc=1, device_id=device(t), device_id_type=MESH)

    for_partners(greet)

    def rows_of(block, count):
        first = block * 8
        return pl.ds(first if isinstance(first, int) else pl.multiple_of(first, 8), count)

    for load in loads[:6]:
        load.wait()

    for level in range(LEVELS):
        for k in range(2):
            send_ph[level, pl.ds(k, 256, stride=2), :] = phase[level, :, k * LANES : (k + 1) * LANES]

    slots = slot[...]
    pair_s[...] = lax.shift_right_logical(slots, 1)
    box_s[...] = (
        move_bits(own[...], ROW_BITS) * 2 + lax.bitwise_and(slots, 1)
    ).astype(F32)
    cosine, sine = cos_sin(ang[...])
    gain = wgt[...] * LEAF_GAIN
    wc_s[...] = gain * cosine
    ws_s[...] = gain * sine
    packed_s[...] = jnp.zeros_like(packed_s)

    row_128 = lax.broadcasted_iota(jnp.int32, (128, LANES), 0)
    row_64 = lax.broadcasted_iota(jnp.int32, (64, LANES), 0)
    row_256f = lax.broadcasted_iota(jnp.int32, (256, LANES), 0).astype(F32)
    before = lax.broadcasted_iota(jnp.int32, (LANES, 256), 0)
    column = lax.broadcasted_iota(jnp.int32, (LANES, 256), 1)
    counter = jnp.where((before < column) | (column >= LANES), 1.0, 0.0).astype(BF)

    def lay_out(block, left, right, counts):
        for j in range(STEP):
            c = block * STEP + j
            lanes = slice(j * LANES, (j + 1) * LANES)
            pair = pair_s[pl.ds(c, 1), :]
            named = row_128 == pair
            seen = dot_nn(jnp.where(named, 1.0, 0.0).astype(BF), counter)
            rank = jnp.sum(
                jnp.where(named, seen[:, :LANES] + counts, 0.0), axis=0, keepdims=True
            )
            counts = counts + seen[:, LANES:]
            high_pair = lax.shift_right_logical(pair, 6).astype(F32) * RANKS
            place = jnp.where(rank < RANKS, high_pair + rank, -1.0)
            right[:, lanes] = jnp.where(row_256f == place, 1.0, 0.0).astype(BF)
            low_pair = row_64 == lax.bitwise_and(pair, 63)
            start = pl.multiple_of(c * LANES, LANES)
            values = (
                split(pos[0:1, pl.ds(start, LANES)], 3)
                + split(pos[1:2, pl.ds(start, LANES)], 3)
                + split(wc_s[pl.ds(c, 1), :], 2)
                + split(ws_s[pl.ds(c, 1), :], 2)
                + [box_s[pl.ds(c, 1), :]]
            )
            for p, value in enumerate(values):
                left[p * 64 : (p + 1) * 64, lanes] = jnp.where(low_pair, value, 0.0).astype(BF)
        return counts

    def gather(left, right):
        packed_s[...] += dot_nt(left[...], right[...])

    def two_blocks(pair, counts):
        counts = lay_out(2 * pair, left_a, right_a, counts)
        gather(left_b, right_b)
        counts = lay_out(2 * pair + 1, left_b, right_b, counts)
        gather(left_a, right_a)
        return counts

    left_b[...] = jnp.zeros_like(left_b)
    right_b[...] = jnp.zeros_like(right_b)
    counts = lax.fori_loop(0, BLOCKS // 2, two_blocks, jnp.zeros((128, LANES), F32))
    gather(left_b, right_b)
    too_many = jnp.max(jnp.max(counts, axis=0, keepdims=True), axis=1, keepdims=True)
    part = 0
    for field, count in enumerate((3, 3, 2, 2, 1)):
        value = packed_s[part * 64 : (part + 1) * 64, :]
        for extra in range(1, count):
            value = value + packed_s[(part + extra) * 64 : (part + extra + 1) * 64, :]
        if field == 0:
            value = jnp.where(too_many > RANKS, 4.0, value)
        part += count
        for half in range(2):
            send_rec[pl.ds(half * 512 + field, 64, stride=8), :] = value[
                :, half * LANES : (half + 1) * LANES
            ]

    pl.semaphore_wait(barrier, DEVICES - 1)

    own_rec = pltpu.make_async_copy(
        send_rec.at[pl.ds(pl.multiple_of(me * 8, 8), FIELDS)],
        recv_rec.at[pl.ds(0, FIELDS)],
        rec_recv.at[0],
    )
    own_rec.start()
    own_ph = pltpu.make_async_copy(
        send_ph.at[:, pl.ds(pl.multiple_of(me * 4, 4), 4)],
        recv_ph.at[:, pl.ds(pl.multiple_of(my_row * 4, 4), 4)],
        own_sem.at[0],
    )
    own_ph.start()

    def send_records(group, j, t, row):
        pltpu.make_async_remote_copy(
            src_ref=send_rec.at[pl.ds(pl.multiple_of(t * 8, 8), FIELDS)],
            dst_ref=recv_rec.at[rows_of(group * GROUP + j, FIELDS)],
            send_sem=rec_send,
            recv_sem=rec_recv.at[group],
            device_id=device(t),
            device_id_type=MESH,
        ).start()

    for_partners(send_records)

    def send_phases(batch):
        levels = BATCHES[batch]

        def send(group, j, t, row):
            pltpu.make_async_remote_copy(
                src_ref=send_ph.at[levels, pl.ds(pl.multiple_of(t * 4, 4), 4)],
                dst_ref=recv_ph.at[levels, pl.ds(pl.multiple_of(my_row * 4, 4), 4)],
                send_sem=ph_send.at[batch],
                recv_sem=ph_recv.at[batch],
                device_id=device(t),
                device_id_type=MESH,
            ).start()

        for_partners(send)

    send_phases(0)

    def wait_for(ref, rows, sem):
        view = ref.at[pl.ds(0, rows)]
        pltpu.make_async_copy(view, view, sem).wait()

    def wait_phases(ref, batch, sems):
        view = ref.at[BATCHES[batch], pl.ds(0, (DEVICES - 1) * 4)]
        pltpu.make_async_copy(view, view, sems.at[batch]).wait()

    leaf_s[...] = jnp.zeros_like(leaf_s)

    def build(group, terms, hot, largest):
        first = pl.multiple_of(group * (GROUP * 8), GROUP * 8)
        field = [recv_rec[pl.ds(first + f, GROUP, stride=8), :] for f in range(FIELDS)]
        for k, value in enumerate(basis_rows(field[1])):
            basis_v[k * GROUP : (k + 1) * GROUP, :] = value
        for k, value in enumerate(basis_rows(field[0])):
            basis_c[k * GROUP : (k + 1) * GROUP, :] = value * field[2]
            basis_s[k * GROUP : (k + 1) * GROUP, :] = value * field[3]
        for s in range(GROUP):
            lanes = slice(s * LANES, (s + 1) * LANES)
            after = slice((GROUP + s) * LANES, (GROUP + s + 1) * LANES)
            second = basis_v[pl.ds(s, Q, stride=GROUP), :]
            for half, basis in enumerate((basis_c, basis_s)):
                for i in range(Q):
                    rows_i = slice(half * POINTS + i * Q, half * POINTS + (i + 1) * Q)
                    term = basis[i * GROUP + s : i * GROUP + s + 1, :] * second
                    high = term.astype(BF)
                    terms[rows_i, lanes] = high
                    terms[rows_i, after] = (term - high.astype(F32)).astype(BF)
            named = jnp.where(row_256f == field[4][s : s + 1, :], 1.0, 0.0).astype(BF)
            hot[:, lanes] = named
            hot[:, after] = named
        return jnp.maximum(largest, field[0])

    def one_group(group, largest):
        @pl.when(group == EARLY)
        def _():
            send_phases(1)

        wait_for(recv_rec, GROUP * FIELDS, rec_recv.at[group])
        largest = build(group, terms_s, hot_s, largest)
        leaf_s[...] += dot_nt(terms_s[...], hot_s[...])
        return largest

    largest = lax.fori_loop(0, GROUPS, one_group, jnp.zeros((GROUP, LANES), F32))
    flag[0, 0] = jnp.max(largest)
    for load in loads[6:]:
        load.wait()
    state_s[...] = leaf_s[...].T

    own_ph.wait()

    def one_level(level, carry):
        for batch, levels in enumerate(BATCHES):

            @pl.when(level == levels.start)
            def _():
                wait_phases(recv_ph, batch, ph_recv)

        for tile in range(32):
            turned = lax.bitwise_and(
                lax.bitwise_or(
                    lax.shift_right_logical(jnp.int32(tile), level),
                    lax.shift_left(jnp.int32(tile), LEVELS - level),
                ),
                31,
            )
            for k in range(2):
                angle_s[tile * 8 : (tile + 1) * 8, k * LANES : (k + 1) * LANES] = recv_ph[
                    level, pl.ds(turned * 16 + k, 8, stride=2), :
                ]
        cosine, sine = cos_sin(angle_s[...])
        real, imag = state_s[:, :POINTS], state_s[:, POINTS:]
        both = []
        for value in (cosine * real - sine * imag, sine * real + cosine * imag):
            both.append(jnp.concatenate([value[:128], value[128:]], axis=1))
        both = jnp.concatenate(both, axis=0)
        high = both.astype(BF)
        low = (both - high.astype(F32)).astype(BF)
        new = dot_nn(high, high_k[...]) + dot_nn(low, high_k[...]) + dot_nn(high, low_k[...])
        for half in range(2):
            part_new = new[half * 128 : (half + 1) * 128].reshape(16, 1, 8, POINTS)
            state_s[:, half * POINTS : (half + 1) * POINTS] = jnp.broadcast_to(
                part_new, (16, 2, 8, POINTS)
            ).reshape(256, POINTS)
        return carry

    lax.fori_loop(0, LEVELS, one_level, 0)

    for k in range(4):
        send_out[pl.ds(k, 256, stride=4), :] = state_s[:, k * LANES : (k + 1) * LANES]
    own_out = pltpu.make_async_copy(
        send_out.at[pl.ds(pl.multiple_of(my_row * 8, 8), 8)],
        out.at[pl.ds(pl.multiple_of(me * 8, 8), 8)],
        own_sem.at[1],
    )
    own_out.start()

    def send_results(group, j, t, row):
        pltpu.make_async_remote_copy(
            src_ref=send_out.at[rows_of(row, 8)],
            dst_ref=out.at[pl.ds(pl.multiple_of(me * 8, 8), 8)],
            send_sem=out_send,
            recv_sem=out_recv,
            device_id=device(t),
            device_id_type=MESH,
        ).start()

    for_partners(send_results)
    own_out.wait()
    wait_for(out, (DEVICES - 1) * 8, out_recv)
    wait_for(send_rec, (DEVICES - 1) * FIELDS, rec_send)
    for batch in range(len(BATCHES)):
        wait_phases(send_ph, batch, ph_send)
    wait_for(send_out, (DEVICES - 1) * 8, out_send)


def fast(positions, angles, weights, owner_dev, leaf_slot, phase_table):
    high_k, low_k = kron_table()
    dma = pltpu.SemaphoreType.DMA
    return pl.pallas_call(
        body,
        out_shape=(
            jax.ShapeDtypeStruct((1024, LANES), F32),
            jax.ShapeDtypeStruct((1, 1), F32),
        ),
        in_specs=[pl.BlockSpec(memory_space=pl.ANY)] * 8,
        out_specs=(
            pl.BlockSpec(memory_space=pl.ANY),
            pl.BlockSpec(memory_space=pltpu.SMEM),
        ),
        scratch_shapes=[
            pltpu.VMEM((2, SOURCES), F32),
            pltpu.VMEM((64, LANES), F32),
            pltpu.VMEM((64, LANES), F32),
            pltpu.VMEM((64, LANES), jnp.int32),
            pltpu.VMEM((64, LANES), jnp.int32),
            pltpu.VMEM((LEVELS, 256, POINTS), F32),
            pltpu.VMEM((512, POINTS), BF),
            pltpu.VMEM((512, POINTS), BF),
            dma((8,)),
            pltpu.VMEM((64, LANES), jnp.int32),
            pltpu.VMEM((64, LANES), F32),
            pltpu.VMEM((64, LANES), F32),
            pltpu.VMEM((64, LANES), F32),
            pltpu.VMEM((PARTS * 64, STEP * LANES), BF),
            pltpu.VMEM((PARTS * 64, STEP * LANES), BF),
            pltpu.VMEM((256, STEP * LANES), BF),
            pltpu.VMEM((256, STEP * LANES), BF),
            pltpu.VMEM((PARTS * 64, 256), F32),
            pltpu.VMEM((1024, LANES), F32),
            pltpu.VMEM((1024, LANES), F32),
            pltpu.VMEM((LEVELS, 512, LANES), F32),
            pltpu.VMEM((LEVELS, 512, LANES), F32),
            pltpu.VMEM((1024, LANES), F32),
            pltpu.VMEM((Q * GROUP, LANES), F32),
            pltpu.VMEM((Q * GROUP, LANES), F32),
            pltpu.VMEM((Q * GROUP, LANES), F32),
            pltpu.VMEM((512, 2 * GROUP * LANES), BF),
            pltpu.VMEM((256, 2 * GROUP * LANES), BF),
            pltpu.VMEM((512, 256), F32),
            pltpu.VMEM((256, 512), F32),
            pltpu.VMEM((256, POINTS), F32),
            dma,
            dma((GROUPS,)),
            dma((len(BATCHES),)),
            dma((len(BATCHES),)),
            dma,
            dma,
            dma((2,)),
        ],
        compiler_params=pltpu.CompilerParams(
            collective_id=0, has_side_effects=True, vmem_limit_bytes=56 << 20
        ),
    )(
        positions,
        angles.reshape(64, LANES),
        weights.reshape(64, LANES),
        owner_dev.reshape(64, LANES),
        leaf_slot.reshape(64, LANES),
        phase_table,
        jnp.asarray(high_k),
        jnp.asarray(low_k),
    )


def shards(*arrays):
    result, largest = fast(*arrays)
    return lax.cond(
        largest[0, 0] > 2.0, plain, lambda *_: result.reshape(256, 512), *arrays
    )


def solution(mesh):
    placed = (
        P(None, ("wide", "narrow")),
        P(("wide", "narrow")),
        P(("wide", "narrow")),
        P(("wide", "narrow"), None),
        P(("wide", "narrow")),
        P(None, ("wide", "narrow"), None),
    )
    return jax.shard_map(
        shards, mesh=mesh, in_specs=placed, out_specs=P(("wide", "narrow"), None), check_vma=False
    )
```

```python
import functools
import math

import jax
import jax.numpy as jnp
import numpy as np
from jax import lax
from jax.experimental import pallas as pl
from jax.experimental.pallas import tpu as pltpu
from jax.sharding import PartitionSpec as P

Q = 16


LEAF_GAIN = 5.0
SQRT_HALF = 0.7071067811865476
HIGH = lax.Precision.HIGHEST
MESH = pl.DeviceIdType.MESH
DEVICES = 128
RANKS = 128
FIELDS = 5
LEVELS = 5
SOURCES = 8192
LANES = 128
POINTS = 256
PARTS = 11
STEP = 8
GROUP = 8
GROUPS = DEVICES // GROUP
BLOCKS = SOURCES // (STEP * LANES)
BATCHES = (slice(0, 5),)
ROW_BITS = ((0, 6), (1, 5), (3, 4), (4, 3), (6, 2), (2, 1), (5, 0))
STEP_BITS = ((6, 6), (5, 2), (4, 0), (3, 5), (2, 1), (1, 4), (0, 3))
BF = jnp.bfloat16
F32 = jnp.float32


def partner_2(value, axis, apart):
    return lax.ppermute(value, axis, [(i, i ^ 1 << apart) for i in range(lax.axis_size(axis))])


def cheb_nodes(grid_order):
    counter = jnp.arange(grid_order, dtype=jnp.float32)
    return jnp.cos((2.0 * counter + 1.0) * math.pi / (2.0 * grid_order))


def lagrange(points, grid_order):
    node_list = cheb_nodes(grid_order)
    offsets = points[..., None] - node_list
    unit_col = jnp.ones_like(offsets[..., :1])
    before = jnp.cumprod(jnp.concatenate([unit_col, offsets[..., :-1]], -1), -1)
    after_prod = jnp.flip(
        jnp.cumprod(jnp.concatenate([unit_col, jnp.flip(offsets[..., 1:], -1)], -1), -1), -1
    )
    node_gaps = node_list[:, None] - node_list[None, :] + jnp.eye(grid_order, dtype=jnp.float32)
    node_prod = jnp.prod(node_gaps, 1)
    return before * after_prod / node_prod


def interp_kron(grid_order, side_value):
    node_list = cheb_nodes(grid_order)
    interp = lagrange((node_list + (2.0 * side_value - 1.0)) * 0.5, grid_order)
    return (interp[:, None, :, None] * interp[None, :, None, :]).reshape(
        grid_order * grid_order, grid_order * grid_order
    )


def apply_kron(coeffs, kron_matrix):
    flat_rows = coeffs.reshape(-1, kron_matrix.shape[0])
    result = lax.dot_general(
        flat_rows,
        kron_matrix,
        (((1,), (1,)), ((), ())),
        precision=HIGH,
        preferred_element_type=jnp.float32,
    )
    return result.reshape(coeffs.shape)


def rotate(coeffs, angle_rows):
    half_width = angle_rows.shape[-1]
    real_part = coeffs[..., :half_width]
    imag_part = coeffs[..., half_width:]
    cosine = jnp.cos(angle_rows)
    sine_val = jnp.sin(angle_rows)
    return jnp.concatenate(
        [cosine * real_part - sine_val * imag_part, sine_val * real_part + cosine * imag_part], -1
    )


def leaf_terms(first_pos, second_pos, phase_angle, weight, grid_order):
    first_basis = lagrange(first_pos, grid_order)
    second_basis = lagrange(second_pos, grid_order)
    outer_prod = (first_basis[:, :, None] * second_basis[:, None, :]).reshape(
        -1, grid_order * grid_order
    ) * (LEAF_GAIN * weight)[:, None]
    return jnp.concatenate(
        [outer_prod * jnp.cos(phase_angle)[:, None], outer_prod * jnp.sin(phase_angle)[:, None]], 1
    )


def combine(own_coeffs, pair_coeffs, side_bit, kron_zero, kron_one):
    kron_own = jnp.where(side_bit == 1, kron_one, kron_zero)
    kron_pair = jnp.where(side_bit == 1, kron_zero, kron_one)
    return SQRT_HALF * (apply_kron(own_coeffs, kron_own) + apply_kron(pair_coeffs, kron_pair))


def plain(positions, angles, weights, owner_dev, leaf_slot, phase_table):
    grid_order = Q
    points_sq = grid_order * grid_order
    wide_count = lax.axis_size("wide")
    narrow_count = lax.axis_size("narrow")
    devices = wide_count * narrow_count
    source_count = angles.shape[0]
    capacity = 4 * source_count // devices
    slot_count = devices * capacity
    box_count = phase_table.shape[1]
    target_dev = owner_dev[:, 0]
    dev_tags = jnp.arange(devices, dtype=jnp.int32)
    dev_counts = jnp.sum((target_dev[:, None] == dev_tags[None, :]).astype(jnp.int32), 0)
    dev_starts = jnp.cumsum(dev_counts) - dev_counts
    source_order = jnp.argsort(target_dev, stable=True)
    rank_grid = jnp.arange(capacity, dtype=jnp.int32)[None, :]
    slot_valid = (rank_grid < dev_counts[:, None]).reshape(slot_count)
    slot_pick = jnp.minimum(dev_starts[:, None] + rank_grid, source_count - 1).reshape(slot_count)
    slot_source = jnp.take(source_order, slot_pick, axis=0)
    records = jnp.stack([positions[0], positions[1], angles, weights])
    float_send = jnp.where(slot_valid[None, :], jnp.take(records, slot_source, axis=1), 0.0)
    index_send = jnp.where(slot_valid, jnp.take(leaf_slot, slot_source, axis=0), 0)[None, :]
    float_recv, index_recv = (
        lax.all_to_all(float_send, ("wide", "narrow"), split_axis=1, concat_axis=1, tiled=True),
        lax.all_to_all(index_send, ("wide", "narrow"), split_axis=1, concat_axis=1, tiled=True),
    )
    block_rows = math.gcd(slot_count, 2048)
    box_tags = jnp.arange(box_count, dtype=jnp.int32)

    def add_block(block_no, running):
        start = block_no * block_rows
        block_recs = lax.dynamic_slice_in_dim(float_recv, start, block_rows, 1)
        block_ids = lax.dynamic_slice_in_dim(index_recv[0], start, block_rows, 0)
        term_rows = leaf_terms(
            block_recs[0], block_recs[1], block_recs[2], block_recs[3], grid_order
        )
        one_hot = (block_ids[:, None] == box_tags[None, :]).astype(jnp.float32)
        return running + lax.dot_general(
            one_hot,
            term_rows,
            (((0,), (0,)), ((), ())),
            precision=HIGH,
            preferred_element_type=jnp.float32,
        )

    coeffs = lax.fori_loop(
        0, slot_count // block_rows, add_block, jnp.zeros((box_count, 2 * points_sq), jnp.float32)
    )
    kron_zero = interp_kron(grid_order, 0.0)
    kron_one = interp_kron(grid_order, 1.0)
    narrow_index = lax.axis_index("narrow")
    wide_index = lax.axis_index("wide")
    for bit_index in (0, 1):
        side_bit = jnp.bitwise_and(jnp.right_shift(narrow_index, bit_index), 1)
        rotated = rotate(coeffs, phase_table[bit_index])
        partner = partner_2(rotated, "narrow", bit_index)
        coeffs = combine(rotated, partner, side_bit, kron_zero, kron_one)
    top_bit = wide_count.bit_length() - 2
    for level_no, bit_index in ((2, 0), (3, 1), (4, top_bit)):
        side_bit = jnp.bitwise_and(jnp.right_shift(wide_index, bit_index), 1)
        rotated = rotate(coeffs, phase_table[level_no])
        partner = partner_2(rotated, "wide", bit_index)
        coeffs = combine(rotated, partner, side_bit, kron_zero, kron_one)
    return coeffs


NODES = np.cos((2 * np.arange(Q) + 1) * np.pi / (2 * Q))
GAPS = np.prod(NODES[:, None] - NODES[None, :] + np.eye(Q), 1)


def kron_table():
    blocks = []
    for side in (0.0, 1.0):
        points = (NODES + 2.0 * side - 1.0) * 0.5
        offsets = points[:, None] - NODES
        basis = np.stack(
            [np.prod(np.delete(offsets, k, 1), 1) / GAPS[k] for k in range(Q)], 1
        )
        blocks.append(np.kron(basis, basis).T)
    table = np.concatenate(blocks, 0) * SQRT_HALF
    high = table.astype(np.float32).astype(BF)
    low = (table - high.astype(np.float64)).astype(np.float32).astype(BF)
    return np.concatenate([high, high, low], 0)


def series(function, degree):
    fit = np.polynomial.chebyshev.Chebyshev.interpolate(
        lambda t: function(np.sqrt(t)), degree, domain=[0.0, np.pi**2]
    )
    return [float(c) for c in fit.convert(kind=np.polynomial.Polynomial).coef]


COS_SERIES = series(np.cos, 6)
SIN_SERIES = series(lambda x: np.sinc(x / np.pi), 6)


def cos_sin(angle):
    square = angle * angle
    cosine = jnp.full_like(angle, COS_SERIES[-1])
    for c in COS_SERIES[-2::-1]:
        cosine = cosine * square + c
    sine = jnp.full_like(angle, SIN_SERIES[-1])
    for c in SIN_SERIES[-2::-1]:
        sine = sine * square + c
    return cosine, sine * angle


def basis_rows(points):
    offsets = [points - float(t) for t in NODES]
    before = [None, offsets[0]]
    for k in range(1, Q - 1):
        before.append(before[-1] * offsets[k])
    after = [None, offsets[Q - 1]]
    for k in range(Q - 2, 0, -1):
        after.append(after[-1] * offsets[k])
    after = after[::-1]
    rows = []
    for k in range(Q):
        scale = float(1.0 / GAPS[k])
        if k == 0:
            rows.append(after[0] * scale)
        elif k == Q - 1:
            rows.append(before[k] * scale)
        else:
            rows.append(before[k] * after[k] * scale)
    return rows


def split(value, count):
    parts = []
    for _ in range(count - 1):
        part = value.astype(BF).astype(F32)
        parts.append(part)
        value = value - part
    return parts + [value]


def move_bits(value, table):
    out = None
    for source, target in table:
        bit = lax.shift_left(
            lax.bitwise_and(lax.shift_right_logical(value, jnp.int32(source)), jnp.int32(1)),
            jnp.int32(target),
        )
        out = bit if out is None else lax.bitwise_or(out, bit)
    return out


def move_bits_of(number, table):
    return sum(((number >> source) & 1) << target for source, target in table)


GROUP_BITS = tuple((step - 3, bit) for step, bit in STEP_BITS if step >= 3)
GROUP_ROW_BITS = tuple((step, dict(ROW_BITS)[bit]) for step, bit in GROUP_BITS)


def dot_nt(left, right):
    return lax.dot_general(left, right, (((1,), (1,)), ((), ())), preferred_element_type=F32)


def dot_nn(left, right):
    return jnp.dot(left, right, preferred_element_type=F32)


def body(
    pos_h, ang_h, wgt_h, own_h, slot_h, phase_h, all_h,
    out, flag,
    pos, ang, wgt, own, slot, phase, all_k, load_sem,
    pair_s, box_s, wc_s, ws_s, left_a, left_b, right_a, right_b, packed_s,
    send_rec, recv_rec, send_ph, recv_ph, send_out,
    basis_v, basis_c, basis_s, terms_s, hot_s, leaf_s, state_s, angle_s,
    rec_send, rec_recv, ph_send, ph_recv, out_send, out_recv, own_sem,
):
    me = lax.axis_index("wide") * 8 + lax.axis_index("narrow")
    my_row = move_bits(me, ROW_BITS)

    def device(t):
        return {"wide": lax.shift_right_logical(t, 3), "narrow": lax.bitwise_and(t, 7)}

    def for_partners(act):
        def visit(group, first):
            base = me if first else lax.bitwise_xor(me, move_bits(group, GROUP_BITS))
            base_row = my_row if first else lax.bitwise_xor(my_row, move_bits(group, GROUP_ROW_BITS))
            for j in range(1 if first else 0, GROUP):
                offset = move_bits_of(j, STEP_BITS)
                act(
                    group,
                    j,
                    lax.bitwise_xor(base, offset),
                    lax.bitwise_xor(base_row, move_bits_of(offset, ROW_BITS)),
                )

        visit(0, True)

        def later(group, carry):
            visit(group, False)
            return carry

        lax.fori_loop(1, GROUPS, later, 0)

    loads = [
        pltpu.make_async_copy(source, target, load_sem.at[i])
        for i, (source, target) in enumerate(
            (
                (phase_h, phase),
                (pos_h, pos),
                (ang_h, ang),
                (wgt_h, wgt),
                (own_h, own),
                (slot_h, slot),
                (all_h, all_k),
            )
        )
    ]
    for load in loads:
        load.start()

    barrier = pltpu.get_barrier_semaphore()

    def greet(group, j, t, row):
        pl.semaphore_signal(barrier, inc=1, device_id=device(t), device_id_type=MESH)

    for_partners(greet)

    def rows_of(block, count):
        first = block * 8
        return pl.ds(first if isinstance(first, int) else pl.multiple_of(first, 8), count)

    for load in loads[1:6]:
        load.wait()

    slots = slot[...]
    pair_s[...] = lax.shift_right_logical(slots, 1)
    box_s[...] = (
        move_bits(own[...], ROW_BITS) * 2 + lax.bitwise_and(slots, 1)
    ).astype(F32)
    cosine, sine = cos_sin(ang[...])
    gain = wgt[...] * LEAF_GAIN
    wc_s[...] = gain * cosine
    ws_s[...] = gain * sine
    packed_s[...] = jnp.zeros_like(packed_s)

    row_128 = lax.broadcasted_iota(jnp.int32, (128, LANES), 0)
    row_64 = lax.broadcasted_iota(jnp.int32, (64, LANES), 0)
    row_256f = lax.broadcasted_iota(jnp.int32, (256, LANES), 0).astype(F32)
    before = lax.broadcasted_iota(jnp.int32, (LANES, 256), 0)
    column = lax.broadcasted_iota(jnp.int32, (LANES, 256), 1)
    counter = jnp.where((before < column) | (column >= LANES), 1.0, 0.0).astype(BF)

    def lay_out(block, left, right, counts):
        for j in range(STEP):
            c = block * STEP + j
            lanes = slice(j * LANES, (j + 1) * LANES)
            pair = pair_s[pl.ds(c, 1), :]
            named = row_128 == pair
            seen = dot_nn(jnp.where(named, 1.0, 0.0).astype(BF), counter)
            rank = jnp.sum(
                jnp.where(named, seen[:, :LANES] + counts, 0.0), axis=0, keepdims=True
            )
            counts = counts + seen[:, LANES:]
            high_pair = lax.shift_right_logical(pair, 6).astype(F32) * RANKS
            place = jnp.where(rank < RANKS, high_pair + rank, -1.0)
            right[:, lanes] = jnp.where(row_256f == place, 1.0, 0.0).astype(BF)
            low_pair = row_64 == lax.bitwise_and(pair, 63)
            start = pl.multiple_of(c * LANES, LANES)
            values = (
                split(pos[0:1, pl.ds(start, LANES)], 3)
                + split(pos[1:2, pl.ds(start, LANES)], 3)
                + split(wc_s[pl.ds(c, 1), :], 2)
                + split(ws_s[pl.ds(c, 1), :], 2)
                + [box_s[pl.ds(c, 1), :]]
            )
            for p, value in enumerate(values):
                left[p * 64 : (p + 1) * 64, lanes] = jnp.where(low_pair, value, 0.0).astype(BF)
        return counts

    def gather(left, right):
        packed_s[...] += dot_nt(left[...], right[...])

    def two_blocks(pair, counts):
        counts = lay_out(2 * pair, left_a, right_a, counts)
        gather(left_b, right_b)
        counts = lay_out(2 * pair + 1, left_b, right_b, counts)
        gather(left_a, right_a)
        return counts

    left_b[...] = jnp.zeros_like(left_b)
    right_b[...] = jnp.zeros_like(right_b)
    counts = lax.fori_loop(0, BLOCKS // 2, two_blocks, jnp.zeros((128, LANES), F32))
    gather(left_b, right_b)
    too_many = jnp.max(jnp.max(counts, axis=0, keepdims=True), axis=1, keepdims=True)
    part = 0
    for field, count in enumerate((3, 3, 2, 2, 1)):
        value = packed_s[part * 64 : (part + 1) * 64, :]
        for extra in range(1, count):
            value = value + packed_s[(part + extra) * 64 : (part + extra + 1) * 64, :]
        if field == 0:
            value = jnp.where(too_many > RANKS, 4.0, value)
        part += count
        for half in range(2):
            send_rec[pl.ds(half * 512 + field, 64, stride=8), :] = value[
                :, half * LANES : (half + 1) * LANES
            ]

    pl.semaphore_wait(barrier, DEVICES - 1)

    own_rec = pltpu.make_async_copy(
        send_rec.at[pl.ds(pl.multiple_of(me * 8, 8), FIELDS)],
        recv_rec.at[pl.ds(0, FIELDS)],
        rec_recv.at[0],
    )
    own_rec.start()
    def send_records(group, j, t, row):
        pltpu.make_async_remote_copy(
            src_ref=send_rec.at[pl.ds(pl.multiple_of(t * 8, 8), FIELDS)],
            dst_ref=recv_rec.at[rows_of(group * GROUP + j, FIELDS)],
            send_sem=rec_send,
            recv_sem=rec_recv.at[group],
            device_id=device(t),
            device_id_type=MESH,
        ).start()

    for_partners(send_records)

    def send_phases(batch):
        levels = BATCHES[batch]

        def send(group, j, t, row):
            pltpu.make_async_remote_copy(
                src_ref=send_ph.at[levels, pl.ds(pl.multiple_of(t * 4, 4), 4)],
                dst_ref=recv_ph.at[levels, pl.ds(pl.multiple_of(my_row * 4, 4), 4)],
                send_sem=ph_send.at[batch],
                recv_sem=ph_recv.at[batch],
                device_id=device(t),
                device_id_type=MESH,
            ).start()

        for_partners(send)

    loads[0].wait()
    for level in range(LEVELS):
        for k in range(2):
            send_ph[level, pl.ds(k, 256, stride=2), :] = phase[level, :, k * LANES : (k + 1) * LANES]

    own_ph = pltpu.make_async_copy(
        send_ph.at[:, pl.ds(pl.multiple_of(me * 4, 4), 4)],
        recv_ph.at[:, pl.ds(pl.multiple_of(my_row * 4, 4), 4)],
        own_sem.at[0],
    )
    own_ph.start()
    send_phases(0)

    def wait_for(ref, rows, sem):
        view = ref.at[pl.ds(0, rows)]
        pltpu.make_async_copy(view, view, sem).wait()

    def wait_phases(ref, batch, sems):
        view = ref.at[BATCHES[batch], pl.ds(0, (DEVICES - 1) * 4)]
        pltpu.make_async_copy(view, view, sems.at[batch]).wait()

    leaf_s[...] = jnp.zeros_like(leaf_s)

    def build(group, terms, hot, largest):
        first = pl.multiple_of(group * (GROUP * 8), GROUP * 8)
        field = [recv_rec[pl.ds(first + f, GROUP, stride=8), :] for f in range(FIELDS)]
        for k, value in enumerate(basis_rows(field[1])):
            basis_v[k * GROUP : (k + 1) * GROUP, :] = value
        for k, value in enumerate(basis_rows(field[0])):
            basis_c[k * GROUP : (k + 1) * GROUP, :] = value * field[2]
            basis_s[k * GROUP : (k + 1) * GROUP, :] = value * field[3]
        for s in range(GROUP):
            lanes = slice(s * LANES, (s + 1) * LANES)
            after = slice((GROUP + s) * LANES, (GROUP + s + 1) * LANES)
            second = basis_v[pl.ds(s, Q, stride=GROUP), :]
            for half, basis in enumerate((basis_c, basis_s)):
                for i in range(Q):
                    rows_i = slice(half * POINTS + i * Q, half * POINTS + (i + 1) * Q)
                    term = basis[i * GROUP + s : i * GROUP + s + 1, :] * second
                    high = term.astype(BF)
                    terms[rows_i, lanes] = high
                    terms[rows_i, after] = (term - high.astype(F32)).astype(BF)
            named = jnp.where(row_256f == field[4][s : s + 1, :], 1.0, 0.0).astype(BF)
            hot[:, lanes] = named
            hot[:, after] = named
        return jnp.maximum(largest, field[0])

    def one_group(group, largest):
        wait_for(recv_rec, GROUP * FIELDS, rec_recv.at[group])
        largest = build(group, terms_s, hot_s, largest)
        leaf_s[...] += dot_nt(terms_s[...], hot_s[...])
        return largest

    largest = lax.fori_loop(0, GROUPS, one_group, jnp.zeros((GROUP, LANES), F32))
    flag[0, 0] = jnp.max(largest)
    for load in loads[6:]:
        load.wait()
    state_s[...] = leaf_s[...].T

    own_ph.wait()

    def one_level(level, carry):
        for batch, levels in enumerate(BATCHES):

            @pl.when(level == levels.start)
            def _():
                wait_phases(recv_ph, batch, ph_recv)

        for tile in range(32):
            turned = lax.bitwise_and(
                lax.bitwise_or(
                    lax.shift_right_logical(jnp.int32(tile), level),
                    lax.shift_left(jnp.int32(tile), LEVELS - level),
                ),
                31,
            )
            for k in range(2):
                angle_s[tile * 8 : (tile + 1) * 8, k * LANES : (k + 1) * LANES] = recv_ph[
                    level, pl.ds(turned * 16 + k, 8, stride=2), :
                ]
        cosine, sine = cos_sin(angle_s[...])
        real, imag = state_s[:, :POINTS], state_s[:, POINTS:]
        both = []
        for value in (cosine * real - sine * imag, sine * real + cosine * imag):
            both.append(jnp.concatenate([value[:128], value[128:]], axis=1))
        both = jnp.concatenate(both, axis=0)
        high = both.astype(BF)
        low = (both - high.astype(F32)).astype(BF)
        new = dot_nn(jnp.concatenate([high, low, high], axis=1), all_k[...])
        for half in range(2):
            part_new = new[half * 128 : (half + 1) * 128].reshape(16, 1, 8, POINTS)
            state_s[:, half * POINTS : (half + 1) * POINTS] = jnp.broadcast_to(
                part_new, (16, 2, 8, POINTS)
            ).reshape(256, POINTS)
        return carry

    lax.fori_loop(0, LEVELS, one_level, 0)

    for k in range(4):
        send_out[pl.ds(k, 256, stride=4), :] = state_s[:, k * LANES : (k + 1) * LANES]
    own_out = pltpu.make_async_copy(
        send_out.at[pl.ds(pl.multiple_of(my_row * 8, 8), 8)],
        out.at[pl.ds(pl.multiple_of(me * 8, 8), 8)],
        own_sem.at[1],
    )
    own_out.start()

    def send_results(group, j, t, row):
        pltpu.make_async_remote_copy(
            src_ref=send_out.at[rows_of(row, 8)],
            dst_ref=out.at[pl.ds(pl.multiple_of(me * 8, 8), 8)],
            send_sem=out_send,
            recv_sem=out_recv,
            device_id=device(t),
            device_id_type=MESH,
        ).start()

    for_partners(send_results)
    own_out.wait()
    wait_for(out, (DEVICES - 1) * 8, out_recv)
    wait_for(send_rec, (DEVICES - 1) * FIELDS, rec_send)
    for batch in range(len(BATCHES)):
        wait_phases(send_ph, batch, ph_send)
    wait_for(send_out, (DEVICES - 1) * 8, out_send)


def fast(positions, angles, weights, owner_dev, leaf_slot, phase_table):
    dma = pltpu.SemaphoreType.DMA
    return pl.pallas_call(
        body,
        out_shape=(
            jax.ShapeDtypeStruct((1024, LANES), F32),
            jax.ShapeDtypeStruct((1, 1), F32),
        ),
        in_specs=[pl.BlockSpec(memory_space=pl.ANY)] * 7,
        out_specs=(
            pl.BlockSpec(memory_space=pl.ANY),
            pl.BlockSpec(memory_space=pltpu.SMEM),
        ),
        scratch_shapes=[
            pltpu.VMEM((2, SOURCES), F32),
            pltpu.VMEM((64, LANES), F32),
            pltpu.VMEM((64, LANES), F32),
            pltpu.VMEM((64, LANES), jnp.int32),
            pltpu.VMEM((64, LANES), jnp.int32),
            pltpu.VMEM((LEVELS, 256, POINTS), F32),
            pltpu.VMEM((1536, POINTS), BF),
            dma((7,)),
            pltpu.VMEM((64, LANES), jnp.int32),
            pltpu.VMEM((64, LANES), F32),
            pltpu.VMEM((64, LANES), F32),
            pltpu.VMEM((64, LANES), F32),
            pltpu.VMEM((PARTS * 64, STEP * LANES), BF),
            pltpu.VMEM((PARTS * 64, STEP * LANES), BF),
            pltpu.VMEM((256, STEP * LANES), BF),
            pltpu.VMEM((256, STEP * LANES), BF),
            pltpu.VMEM((PARTS * 64, 256), F32),
            pltpu.VMEM((1024, LANES), F32),
            pltpu.VMEM((1024, LANES), F32),
            pltpu.VMEM((LEVELS, 512, LANES), F32),
            pltpu.VMEM((LEVELS, 512, LANES), F32),
            pltpu.VMEM((1024, LANES), F32),
            pltpu.VMEM((Q * GROUP, LANES), F32),
            pltpu.VMEM((Q * GROUP, LANES), F32),
            pltpu.VMEM((Q * GROUP, LANES), F32),
            pltpu.VMEM((512, 2 * GROUP * LANES), BF),
            pltpu.VMEM((256, 2 * GROUP * LANES), BF),
            pltpu.VMEM((512, 256), F32),
            pltpu.VMEM((256, 512), F32),
            pltpu.VMEM((256, POINTS), F32),
            dma,
            dma((GROUPS,)),
            dma((len(BATCHES),)),
            dma((len(BATCHES),)),
            dma,
            dma,
            dma((2,)),
        ],
        compiler_params=pltpu.CompilerParams(
            collective_id=0, has_side_effects=True, vmem_limit_bytes=56 << 20
        ),
    )(
        positions,
        angles.reshape(64, LANES),
        weights.reshape(64, LANES),
        owner_dev.reshape(64, LANES),
        leaf_slot.reshape(64, LANES),
        phase_table,
        jnp.asarray(kron_table()),
    )


def shards(*arrays):
    result, largest = fast(*arrays)
    return lax.cond(
        largest[0, 0] > 2.0, plain, lambda *_: result.reshape(256, 512), *arrays
    )


def solution(mesh):
    placed = (
        P(None, ("wide", "narrow")),
        P(("wide", "narrow")),
        P(("wide", "narrow")),
        P(("wide", "narrow"), None),
        P(("wide", "narrow")),
        P(None, ("wide", "narrow"), None),
    )
    return jax.shard_map(
        shards, mesh=mesh, in_specs=placed, out_specs=P(("wide", "narrow"), None), check_vma=False
    )
```

```python
import functools
import math

import jax
import jax.numpy as jnp
import numpy as np
from jax import lax
from jax.experimental import pallas as pl
from jax.experimental.pallas import tpu as pltpu
from jax.sharding import PartitionSpec as P

Q = 16


LEAF_GAIN = 5.0
SQRT_HALF = 0.7071067811865476
HIGH = lax.Precision.HIGHEST
MESH = pl.DeviceIdType.MESH
DEVICES = 128
RANKS = 128
FIELDS = 5
LEVELS = 5
SOURCES = 8192
LANES = 128
POINTS = 256
PARTS = 11
STEP = 8
GROUP = 8
GROUPS = DEVICES // GROUP
BLOCKS = SOURCES // (STEP * LANES)
BATCHES = (slice(0, 5),)
ROW_BITS = ((0, 6), (1, 5), (3, 4), (4, 3), (6, 2), (2, 1), (5, 0))
STEP_BITS = ((6, 6), (5, 2), (4, 0), (3, 5), (2, 1), (1, 4), (0, 3))
BF = jnp.bfloat16
F32 = jnp.float32


def partner_2(value, axis, apart):
    return lax.ppermute(value, axis, [(i, i ^ 1 << apart) for i in range(lax.axis_size(axis))])


def cheb_nodes(grid_order):
    counter = jnp.arange(grid_order, dtype=jnp.float32)
    return jnp.cos((2.0 * counter + 1.0) * math.pi / (2.0 * grid_order))


def lagrange(points, grid_order):
    node_list = cheb_nodes(grid_order)
    offsets = points[..., None] - node_list
    unit_col = jnp.ones_like(offsets[..., :1])
    before = jnp.cumprod(jnp.concatenate([unit_col, offsets[..., :-1]], -1), -1)
    after_prod = jnp.flip(
        jnp.cumprod(jnp.concatenate([unit_col, jnp.flip(offsets[..., 1:], -1)], -1), -1), -1
    )
    node_gaps = node_list[:, None] - node_list[None, :] + jnp.eye(grid_order, dtype=jnp.float32)
    node_prod = jnp.prod(node_gaps, 1)
    return before * after_prod / node_prod


def interp_kron(grid_order, side_value):
    node_list = cheb_nodes(grid_order)
    interp = lagrange((node_list + (2.0 * side_value - 1.0)) * 0.5, grid_order)
    return (interp[:, None, :, None] * interp[None, :, None, :]).reshape(
        grid_order * grid_order, grid_order * grid_order
    )


def apply_kron(coeffs, kron_matrix):
    flat_rows = coeffs.reshape(-1, kron_matrix.shape[0])
    result = lax.dot_general(
        flat_rows,
        kron_matrix,
        (((1,), (1,)), ((), ())),
        precision=HIGH,
        preferred_element_type=jnp.float32,
    )
    return result.reshape(coeffs.shape)


def rotate(coeffs, angle_rows):
    half_width = angle_rows.shape[-1]
    real_part = coeffs[..., :half_width]
    imag_part = coeffs[..., half_width:]
    cosine = jnp.cos(angle_rows)
    sine_val = jnp.sin(angle_rows)
    return jnp.concatenate(
        [cosine * real_part - sine_val * imag_part, sine_val * real_part + cosine * imag_part], -1
    )


def leaf_terms(first_pos, second_pos, phase_angle, weight, grid_order):
    first_basis = lagrange(first_pos, grid_order)
    second_basis = lagrange(second_pos, grid_order)
    outer_prod = (first_basis[:, :, None] * second_basis[:, None, :]).reshape(
        -1, grid_order * grid_order
    ) * (LEAF_GAIN * weight)[:, None]
    return jnp.concatenate(
        [outer_prod * jnp.cos(phase_angle)[:, None], outer_prod * jnp.sin(phase_angle)[:, None]], 1
    )


def combine(own_coeffs, pair_coeffs, side_bit, kron_zero, kron_one):
    kron_own = jnp.where(side_bit == 1, kron_one, kron_zero)
    kron_pair = jnp.where(side_bit == 1, kron_zero, kron_one)
    return SQRT_HALF * (apply_kron(own_coeffs, kron_own) + apply_kron(pair_coeffs, kron_pair))


def plain(positions, angles, weights, owner_dev, leaf_slot, phase_table):
    grid_order = Q
    points_sq = grid_order * grid_order
    wide_count = lax.axis_size("wide")
    narrow_count = lax.axis_size("narrow")
    devices = wide_count * narrow_count
    source_count = angles.shape[0]
    capacity = 4 * source_count // devices
    slot_count = devices * capacity
    box_count = phase_table.shape[1]
    target_dev = owner_dev[:, 0]
    dev_tags = jnp.arange(devices, dtype=jnp.int32)
    dev_counts = jnp.sum((target_dev[:, None] == dev_tags[None, :]).astype(jnp.int32), 0)
    dev_starts = jnp.cumsum(dev_counts) - dev_counts
    source_order = jnp.argsort(target_dev, stable=True)
    rank_grid = jnp.arange(capacity, dtype=jnp.int32)[None, :]
    slot_valid = (rank_grid < dev_counts[:, None]).reshape(slot_count)
    slot_pick = jnp.minimum(dev_starts[:, None] + rank_grid, source_count - 1).reshape(slot_count)
    slot_source = jnp.take(source_order, slot_pick, axis=0)
    records = jnp.stack([positions[0], positions[1], angles, weights])
    float_send = jnp.where(slot_valid[None, :], jnp.take(records, slot_source, axis=1), 0.0)
    index_send = jnp.where(slot_valid, jnp.take(leaf_slot, slot_source, axis=0), 0)[None, :]
    float_recv, index_recv = (
        lax.all_to_all(float_send, ("wide", "narrow"), split_axis=1, concat_axis=1, tiled=True),
        lax.all_to_all(index_send, ("wide", "narrow"), split_axis=1, concat_axis=1, tiled=True),
    )
    block_rows = math.gcd(slot_count, 2048)
    box_tags = jnp.arange(box_count, dtype=jnp.int32)

    def add_block(block_no, running):
        start = block_no * block_rows
        block_recs = lax.dynamic_slice_in_dim(float_recv, start, block_rows, 1)
        block_ids = lax.dynamic_slice_in_dim(index_recv[0], start, block_rows, 0)
        term_rows = leaf_terms(
            block_recs[0], block_recs[1], block_recs[2], block_recs[3], grid_order
        )
        one_hot = (block_ids[:, None] == box_tags[None, :]).astype(jnp.float32)
        return running + lax.dot_general(
            one_hot,
            term_rows,
            (((0,), (0,)), ((), ())),
            precision=HIGH,
            preferred_element_type=jnp.float32,
        )

    coeffs = lax.fori_loop(
        0, slot_count // block_rows, add_block, jnp.zeros((box_count, 2 * points_sq), jnp.float32)
    )
    kron_zero = interp_kron(grid_order, 0.0)
    kron_one = interp_kron(grid_order, 1.0)
    narrow_index = lax.axis_index("narrow")
    wide_index = lax.axis_index("wide")
    for bit_index in (0, 1):
        side_bit = jnp.bitwise_and(jnp.right_shift(narrow_index, bit_index), 1)
        rotated = rotate(coeffs, phase_table[bit_index])
        partner = partner_2(rotated, "narrow", bit_index)
        coeffs = combine(rotated, partner, side_bit, kron_zero, kron_one)
    top_bit = wide_count.bit_length() - 2
    for level_no, bit_index in ((2, 0), (3, 1), (4, top_bit)):
        side_bit = jnp.bitwise_and(jnp.right_shift(wide_index, bit_index), 1)
        rotated = rotate(coeffs, phase_table[level_no])
        partner = partner_2(rotated, "wide", bit_index)
        coeffs = combine(rotated, partner, side_bit, kron_zero, kron_one)
    return coeffs


NODES = np.cos((2 * np.arange(Q) + 1) * np.pi / (2 * Q))
GAPS = np.prod(NODES[:, None] - NODES[None, :] + np.eye(Q), 1)


def kron_table():
    blocks = []
    for side in (0.0, 1.0):
        points = (NODES + 2.0 * side - 1.0) * 0.5
        offsets = points[:, None] - NODES
        basis = np.stack(
            [np.prod(np.delete(offsets, k, 1), 1) / GAPS[k] for k in range(Q)], 1
        )
        blocks.append(np.kron(basis, basis).T)
    table = np.concatenate(blocks, 0) * SQRT_HALF
    high = table.astype(np.float32).astype(BF)
    low = (table - high.astype(np.float64)).astype(np.float32).astype(BF)
    return np.concatenate([high, high, low], 0)


def series(function, degree):
    fit = np.polynomial.chebyshev.Chebyshev.interpolate(
        lambda t: function(np.sqrt(t)), degree, domain=[0.0, np.pi**2]
    )
    return [float(c) for c in fit.convert(kind=np.polynomial.Polynomial).coef]


COS_SERIES = series(np.cos, 6)
SIN_SERIES = series(lambda x: np.sinc(x / np.pi), 6)


def cos_sin(angle):
    square = angle * angle
    cosine = jnp.full_like(angle, COS_SERIES[-1])
    for c in COS_SERIES[-2::-1]:
        cosine = cosine * square + c
    sine = jnp.full_like(angle, SIN_SERIES[-1])
    for c in SIN_SERIES[-2::-1]:
        sine = sine * square + c
    return cosine, sine * angle


def basis_rows(points):
    offsets = [points - float(t) for t in NODES]
    before = [None, offsets[0]]
    for k in range(1, Q - 1):
        before.append(before[-1] * offsets[k])
    after = [None, offsets[Q - 1]]
    for k in range(Q - 2, 0, -1):
        after.append(after[-1] * offsets[k])
    after = after[::-1]
    rows = []
    for k in range(Q):
        scale = float(1.0 / GAPS[k])
        if k == 0:
            rows.append(after[0] * scale)
        elif k == Q - 1:
            rows.append(before[k] * scale)
        else:
            rows.append(before[k] * after[k] * scale)
    return rows


def split(value, count):
    parts = []
    for _ in range(count - 1):
        part = value.astype(BF).astype(F32)
        parts.append(part)
        value = value - part
    return parts + [value]


def move_bits(value, table):
    out = None
    for source, target in table:
        bit = lax.shift_left(
            lax.bitwise_and(lax.shift_right_logical(value, jnp.int32(source)), jnp.int32(1)),
            jnp.int32(target),
        )
        out = bit if out is None else lax.bitwise_or(out, bit)
    return out


def move_bits_of(number, table):
    return sum(((number >> source) & 1) << target for source, target in table)


GROUP_BITS = tuple((step - 3, bit) for step, bit in STEP_BITS if step >= 3)
GROUP_ROW_BITS = tuple((step, dict(ROW_BITS)[bit]) for step, bit in GROUP_BITS)


def dot_nt(left, right):
    return lax.dot_general(left, right, (((1,), (1,)), ((), ())), preferred_element_type=F32)


def dot_nn(left, right):
    return jnp.dot(left, right, preferred_element_type=F32)


def body(
    pos_h, ang_h, wgt_h, own_h, slot_h, phase_h, all_h,
    out, flag,
    pos, ang, wgt, own, slot, phase, all_k, load_sem,
    pair_s, box_s, wc_s, ws_s, left_a, left_b, right_a, right_b, packed_s,
    send_rec, recv_rec, send_ph, recv_ph, send_out,
    basis_v, basis_c, basis_s, terms_s, hot_s, leaf_s, state_s, angle_s,
    rec_send, rec_recv, ph_send, ph_recv, out_send, out_recv, own_sem,
):
    me = lax.axis_index("wide") * 8 + lax.axis_index("narrow")
    my_row = move_bits(me, ROW_BITS)

    def device(t):
        return {"wide": lax.shift_right_logical(t, 3), "narrow": lax.bitwise_and(t, 7)}

    def for_partners(act):
        def visit(group, first):
            base = me if first else lax.bitwise_xor(me, move_bits(group, GROUP_BITS))
            base_row = my_row if first else lax.bitwise_xor(my_row, move_bits(group, GROUP_ROW_BITS))
            for j in range(1 if first else 0, GROUP):
                offset = move_bits_of(j, STEP_BITS)
                act(
                    group,
                    j,
                    lax.bitwise_xor(base, offset),
                    lax.bitwise_xor(base_row, move_bits_of(offset, ROW_BITS)),
                )

        visit(0, True)

        def later(group, carry):
            visit(group, False)
            return carry

        lax.fori_loop(1, GROUPS, later, 0)

    loads = [
        pltpu.make_async_copy(source, target, load_sem.at[i])
        for i, (source, target) in enumerate(
            (
                (phase_h, phase),
                (pos_h, pos),
                (ang_h, ang),
                (wgt_h, wgt),
                (own_h, own),
                (slot_h, slot),
                (all_h, all_k),
            )
        )
    ]
    for load in loads:
        load.start()

    barrier = pltpu.get_barrier_semaphore()

    def greet(group, j, t, row):
        pl.semaphore_signal(barrier, inc=1, device_id=device(t), device_id_type=MESH)

    for_partners(greet)

    def rows_of(block, count):
        first = block * 8
        return pl.ds(first if isinstance(first, int) else pl.multiple_of(first, 8), count)

    for load in loads[1:6]:
        load.wait()

    slots = slot[...]
    pair_s[...] = lax.shift_right_logical(slots, 1)
    box_s[...] = (
        move_bits(own[...], ROW_BITS) * 2 + lax.bitwise_and(slots, 1)
    ).astype(F32)
    cosine, sine = cos_sin(ang[...])
    gain = wgt[...] * LEAF_GAIN
    wc_s[...] = gain * cosine
    ws_s[...] = gain * sine
    packed_s[...] = jnp.zeros_like(packed_s)

    row_128 = lax.broadcasted_iota(jnp.int32, (128, LANES), 0)
    row_64 = lax.broadcasted_iota(jnp.int32, (64, LANES), 0).astype(F32).astype(BF)
    row_256 = lax.broadcasted_iota(jnp.int32, (256, LANES), 0).astype(F32).astype(BF)
    one, zero = jnp.asarray(1.0, BF), jnp.asarray(0.0, BF)
    before = lax.broadcasted_iota(jnp.int32, (LANES, 256), 0)
    column = lax.broadcasted_iota(jnp.int32, (LANES, 256), 1)
    counter = jnp.where((before < column) | (column >= LANES), 1.0, 0.0).astype(BF)

    def lay_out(block, left, right, counts):
        for j in range(STEP):
            c = block * STEP + j
            lanes = slice(j * LANES, (j + 1) * LANES)
            pair = pair_s[pl.ds(c, 1), :]
            named = row_128 == pair
            seen = dot_nn(jnp.where(named, 1.0, 0.0).astype(BF), counter)
            rank = jnp.sum(
                jnp.where(named, seen[:, :LANES] + counts, 0.0), axis=0, keepdims=True
            )
            counts = counts + seen[:, LANES:]
            high_pair = lax.shift_right_logical(pair, 6).astype(F32) * RANKS
            place = jnp.where(rank < RANKS, high_pair + rank, -1.0)
            right[:, lanes] = jnp.where(row_256 == place.astype(BF), one, zero)
            low_pair = row_64 == lax.bitwise_and(pair, 63).astype(F32).astype(BF)
            start = pl.multiple_of(c * LANES, LANES)
            values = (
                split(pos[0:1, pl.ds(start, LANES)], 3)
                + split(pos[1:2, pl.ds(start, LANES)], 3)
                + split(wc_s[pl.ds(c, 1), :], 2)
                + split(ws_s[pl.ds(c, 1), :], 2)
                + [box_s[pl.ds(c, 1), :]]
            )
            for p, value in enumerate(values):
                left[p * 64 : (p + 1) * 64, lanes] = jnp.where(low_pair, value.astype(BF), zero)
        return counts

    def gather(left, right):
        packed_s[...] += dot_nt(left[...], right[...])

    def two_blocks(pair, counts):
        counts = lay_out(2 * pair, left_a, right_a, counts)
        gather(left_b, right_b)
        counts = lay_out(2 * pair + 1, left_b, right_b, counts)
        gather(left_a, right_a)
        return counts

    left_b[...] = jnp.zeros_like(left_b)
    right_b[...] = jnp.zeros_like(right_b)
    counts = lax.fori_loop(0, BLOCKS // 2, two_blocks, jnp.zeros((128, LANES), F32))
    gather(left_b, right_b)
    too_many = jnp.max(jnp.max(counts, axis=0, keepdims=True), axis=1, keepdims=True)
    part = 0
    for field, count in enumerate((3, 3, 2, 2, 1)):
        value = packed_s[part * 64 : (part + 1) * 64, :]
        for extra in range(1, count):
            value = value + packed_s[(part + extra) * 64 : (part + extra + 1) * 64, :]
        if field == 0:
            value = jnp.where(too_many > RANKS, 4.0, value)
        part += count
        for half in range(2):
            send_rec[pl.ds(half * 512 + field, 64, stride=8), :] = value[
                :, half * LANES : (half + 1) * LANES
            ]

    pl.semaphore_wait(barrier, DEVICES - 1)

    own_rec = pltpu.make_async_copy(
        send_rec.at[pl.ds(pl.multiple_of(me * 8, 8), FIELDS)],
        recv_rec.at[pl.ds(0, FIELDS)],
        rec_recv.at[0],
    )
    own_rec.start()
    def send_records(group, j, t, row):
        pltpu.make_async_remote_copy(
            src_ref=send_rec.at[pl.ds(pl.multiple_of(t * 8, 8), FIELDS)],
            dst_ref=recv_rec.at[rows_of(group * GROUP + j, FIELDS)],
            send_sem=rec_send,
            recv_sem=rec_recv.at[group],
            device_id=device(t),
            device_id_type=MESH,
        ).start()

    for_partners(send_records)

    def send_phases(batch):
        levels = BATCHES[batch]

        def send(group, j, t, row):
            pltpu.make_async_remote_copy(
                src_ref=send_ph.at[levels, pl.ds(pl.multiple_of(t * 4, 4), 4)],
                dst_ref=recv_ph.at[levels, pl.ds(pl.multiple_of(my_row * 4, 4), 4)],
                send_sem=ph_send.at[batch],
                recv_sem=ph_recv.at[batch],
                device_id=device(t),
                device_id_type=MESH,
            ).start()

        for_partners(send)

    loads[0].wait()
    for level in range(LEVELS):
        for k in range(2):
            send_ph[level, pl.ds(k, 256, stride=2), :] = phase[level, :, k * LANES : (k + 1) * LANES]

    own_ph = pltpu.make_async_copy(
        send_ph.at[:, pl.ds(pl.multiple_of(me * 4, 4), 4)],
        recv_ph.at[:, pl.ds(pl.multiple_of(my_row * 4, 4), 4)],
        own_sem.at[0],
    )
    own_ph.start()
    send_phases(0)

    def wait_for(ref, rows, sem):
        view = ref.at[pl.ds(0, rows)]
        pltpu.make_async_copy(view, view, sem).wait()

    def wait_phases(ref, batch, sems):
        view = ref.at[BATCHES[batch], pl.ds(0, (DEVICES - 1) * 4)]
        pltpu.make_async_copy(view, view, sems.at[batch]).wait()

    leaf_s[...] = jnp.zeros_like(leaf_s)

    def build(group, terms, hot, largest):
        first = pl.multiple_of(group * (GROUP * 8), GROUP * 8)
        field = [recv_rec[pl.ds(first + f, GROUP, stride=8), :] for f in range(FIELDS)]
        for k, value in enumerate(basis_rows(field[1])):
            basis_v[k * GROUP : (k + 1) * GROUP, :] = value
        for k, value in enumerate(basis_rows(field[0])):
            basis_c[k * GROUP : (k + 1) * GROUP, :] = value * field[2]
            basis_s[k * GROUP : (k + 1) * GROUP, :] = value * field[3]
        for s in range(GROUP):
            lanes = slice(s * LANES, (s + 1) * LANES)
            after = slice((GROUP + s) * LANES, (GROUP + s + 1) * LANES)
            second = basis_v[pl.ds(s, Q, stride=GROUP), :]
            for half, basis in enumerate((basis_c, basis_s)):
                for i in range(Q):
                    rows_i = slice(half * POINTS + i * Q, half * POINTS + (i + 1) * Q)
                    term = basis[i * GROUP + s : i * GROUP + s + 1, :] * second
                    high = term.astype(BF)
                    terms[rows_i, lanes] = high
                    terms[rows_i, after] = (term - high.astype(F32)).astype(BF)
            hot[:, lanes] = jnp.where(row_256 == field[4][s : s + 1, :].astype(BF), one, zero)
        return jnp.maximum(largest, field[0])

    def one_group(group, largest):
        wait_for(recv_rec, GROUP * FIELDS, rec_recv.at[group])
        largest = build(group, terms_s, hot_s, largest)
        width = GROUP * LANES
        leaf_s[...] += dot_nt(terms_s[:, :width], hot_s[...]) + dot_nt(
            terms_s[:, width:], hot_s[...]
        )
        return largest

    largest = lax.fori_loop(0, GROUPS, one_group, jnp.zeros((GROUP, LANES), F32))
    flag[0, 0] = jnp.max(largest)
    for load in loads[6:]:
        load.wait()
    state_s[...] = leaf_s[...].T

    own_ph.wait()

    def one_level(level, carry):
        for batch, levels in enumerate(BATCHES):

            @pl.when(level == levels.start)
            def _():
                wait_phases(recv_ph, batch, ph_recv)

        for tile in range(32):
            turned = lax.bitwise_and(
                lax.bitwise_or(
                    lax.shift_right_logical(jnp.int32(tile), level),
                    lax.shift_left(jnp.int32(tile), LEVELS - level),
                ),
                31,
            )
            for k in range(2):
                angle_s[tile * 8 : (tile + 1) * 8, k * LANES : (k + 1) * LANES] = recv_ph[
                    level, pl.ds(turned * 16 + k, 8, stride=2), :
                ]
        cosine, sine = cos_sin(angle_s[...])
        real, imag = state_s[:, :POINTS], state_s[:, POINTS:]
        both = []
        for value in (cosine * real - sine * imag, sine * real + cosine * imag):
            both.append(jnp.concatenate([value[:128], value[128:]], axis=1))
        both = jnp.concatenate(both, axis=0)
        high = both.astype(BF)
        low = (both - high.astype(F32)).astype(BF)
        new = dot_nn(jnp.concatenate([high, low, high], axis=1), all_k[...])
        for half in range(2):
            part_new = new[half * 128 : (half + 1) * 128].reshape(16, 1, 8, POINTS)
            state_s[:, half * POINTS : (half + 1) * POINTS] = jnp.broadcast_to(
                part_new, (16, 2, 8, POINTS)
            ).reshape(256, POINTS)
        return carry

    lax.fori_loop(0, LEVELS, one_level, 0)

    for k in range(4):
        send_out[pl.ds(k, 256, stride=4), :] = state_s[:, k * LANES : (k + 1) * LANES]
    own_out = pltpu.make_async_copy(
        send_out.at[pl.ds(pl.multiple_of(my_row * 8, 8), 8)],
        out.at[pl.ds(pl.multiple_of(me * 8, 8), 8)],
        own_sem.at[1],
    )
    own_out.start()

    def send_results(group, j, t, row):
        pltpu.make_async_remote_copy(
            src_ref=send_out.at[rows_of(row, 8)],
            dst_ref=out.at[pl.ds(pl.multiple_of(me * 8, 8), 8)],
            send_sem=out_send,
            recv_sem=out_recv,
            device_id=device(t),
            device_id_type=MESH,
        ).start()

    for_partners(send_results)
    own_out.wait()
    wait_for(out, (DEVICES - 1) * 8, out_recv)
    wait_for(send_rec, (DEVICES - 1) * FIELDS, rec_send)
    for batch in range(len(BATCHES)):
        wait_phases(send_ph, batch, ph_send)
    wait_for(send_out, (DEVICES - 1) * 8, out_send)


def fast(positions, angles, weights, owner_dev, leaf_slot, phase_table):
    dma = pltpu.SemaphoreType.DMA
    return pl.pallas_call(
        body,
        out_shape=(
            jax.ShapeDtypeStruct((1024, LANES), F32),
            jax.ShapeDtypeStruct((1, 1), F32),
        ),
        in_specs=[pl.BlockSpec(memory_space=pl.ANY)] * 7,
        out_specs=(
            pl.BlockSpec(memory_space=pl.ANY),
            pl.BlockSpec(memory_space=pltpu.SMEM),
        ),
        scratch_shapes=[
            pltpu.VMEM((2, SOURCES), F32),
            pltpu.VMEM((64, LANES), F32),
            pltpu.VMEM((64, LANES), F32),
            pltpu.VMEM((64, LANES), jnp.int32),
            pltpu.VMEM((64, LANES), jnp.int32),
            pltpu.VMEM((LEVELS, 256, POINTS), F32),
            pltpu.VMEM((1536, POINTS), BF),
            dma((7,)),
            pltpu.VMEM((64, LANES), jnp.int32),
            pltpu.VMEM((64, LANES), F32),
            pltpu.VMEM((64, LANES), F32),
            pltpu.VMEM((64, LANES), F32),
            pltpu.VMEM((PARTS * 64, STEP * LANES), BF),
            pltpu.VMEM((PARTS * 64, STEP * LANES), BF),
            pltpu.VMEM((256, STEP * LANES), BF),
            pltpu.VMEM((256, STEP * LANES), BF),
            pltpu.VMEM((PARTS * 64, 256), F32),
            pltpu.VMEM((1024, LANES), F32),
            pltpu.VMEM((1024, LANES), F32),
            pltpu.VMEM((LEVELS, 512, LANES), F32),
            pltpu.VMEM((LEVELS, 512, LANES), F32),
            pltpu.VMEM((1024, LANES), F32),
            pltpu.VMEM((Q * GROUP, LANES), F32),
            pltpu.VMEM((Q * GROUP, LANES), F32),
            pltpu.VMEM((Q * GROUP, LANES), F32),
            pltpu.VMEM((512, 2 * GROUP * LANES), BF),
            pltpu.VMEM((256, GROUP * LANES), BF),
            pltpu.VMEM((512, 256), F32),
            pltpu.VMEM((256, 512), F32),
            pltpu.VMEM((256, POINTS), F32),
            dma,
            dma((GROUPS,)),
            dma((len(BATCHES),)),
            dma((len(BATCHES),)),
            dma,
            dma,
            dma((2,)),
        ],
        compiler_params=pltpu.CompilerParams(
            collective_id=0, has_side_effects=True, vmem_limit_bytes=56 << 20
        ),
    )(
        positions,
        angles.reshape(64, LANES),
        weights.reshape(64, LANES),
        owner_dev.reshape(64, LANES),
        leaf_slot.reshape(64, LANES),
        phase_table,
        jnp.asarray(kron_table()),
    )


def shards(*arrays):
    result, largest = fast(*arrays)
    return lax.cond(
        largest[0, 0] > 2.0, plain, lambda *_: result.reshape(256, 512), *arrays
    )


def solution(mesh):
    placed = (
        P(None, ("wide", "narrow")),
        P(("wide", "narrow")),
        P(("wide", "narrow")),
        P(("wide", "narrow"), None),
        P(("wide", "narrow")),
        P(None, ("wide", "narrow"), None),
    )
    return jax.shard_map(
        shards, mesh=mesh, in_specs=placed, out_specs=P(("wide", "narrow"), None), check_vma=False
    )
```

```python
import functools
import math

import jax
import jax.numpy as jnp
import numpy as np
from jax import lax
from jax.experimental import pallas as pl
from jax.experimental.pallas import tpu as pltpu
from jax.sharding import PartitionSpec as P

Q = 16


LEAF_GAIN = 5.0
SQRT_HALF = 0.7071067811865476
HIGH = lax.Precision.HIGHEST
MESH = pl.DeviceIdType.MESH
DEVICES = 128
RANKS = 128
FIELDS = 5
LEVELS = 5
SOURCES = 8192
LANES = 128
POINTS = 256
PARTS = 11
STEP = 8
GROUP = 8
GROUPS = DEVICES // GROUP
BLOCKS = SOURCES // (STEP * LANES)
BATCHES = (slice(0, 5),)
ROW_BITS = ((0, 6), (1, 5), (3, 4), (4, 3), (6, 2), (2, 1), (5, 0))
STEP_BITS = ((6, 6), (5, 2), (4, 0), (3, 5), (2, 1), (1, 4), (0, 3))
MIXED_BITS = ((6, 3), (5, 4), (4, 1), (3, 5), (2, 0), (1, 2), (0, 6))
BF = jnp.bfloat16
F32 = jnp.float32


def partner_2(value, axis, apart):
    return lax.ppermute(value, axis, [(i, i ^ 1 << apart) for i in range(lax.axis_size(axis))])


def cheb_nodes(grid_order):
    counter = jnp.arange(grid_order, dtype=jnp.float32)
    return jnp.cos((2.0 * counter + 1.0) * math.pi / (2.0 * grid_order))


def lagrange(points, grid_order):
    node_list = cheb_nodes(grid_order)
    offsets = points[..., None] - node_list
    unit_col = jnp.ones_like(offsets[..., :1])
    before = jnp.cumprod(jnp.concatenate([unit_col, offsets[..., :-1]], -1), -1)
    after_prod = jnp.flip(
        jnp.cumprod(jnp.concatenate([unit_col, jnp.flip(offsets[..., 1:], -1)], -1), -1), -1
    )
    node_gaps = node_list[:, None] - node_list[None, :] + jnp.eye(grid_order, dtype=jnp.float32)
    node_prod = jnp.prod(node_gaps, 1)
    return before * after_prod / node_prod


def interp_kron(grid_order, side_value):
    node_list = cheb_nodes(grid_order)
    interp = lagrange((node_list + (2.0 * side_value - 1.0)) * 0.5, grid_order)
    return (interp[:, None, :, None] * interp[None, :, None, :]).reshape(
        grid_order * grid_order, grid_order * grid_order
    )


def apply_kron(coeffs, kron_matrix):
    flat_rows = coeffs.reshape(-1, kron_matrix.shape[0])
    result = lax.dot_general(
        flat_rows,
        kron_matrix,
        (((1,), (1,)), ((), ())),
        precision=HIGH,
        preferred_element_type=jnp.float32,
    )
    return result.reshape(coeffs.shape)


def rotate(coeffs, angle_rows):
    half_width = angle_rows.shape[-1]
    real_part = coeffs[..., :half_width]
    imag_part = coeffs[..., half_width:]
    cosine = jnp.cos(angle_rows)
    sine_val = jnp.sin(angle_rows)
    return jnp.concatenate(
        [cosine * real_part - sine_val * imag_part, sine_val * real_part + cosine * imag_part], -1
    )


def leaf_terms(first_pos, second_pos, phase_angle, weight, grid_order):
    first_basis = lagrange(first_pos, grid_order)
    second_basis = lagrange(second_pos, grid_order)
    outer_prod = (first_basis[:, :, None] * second_basis[:, None, :]).reshape(
        -1, grid_order * grid_order
    ) * (LEAF_GAIN * weight)[:, None]
    return jnp.concatenate(
        [outer_prod * jnp.cos(phase_angle)[:, None], outer_prod * jnp.sin(phase_angle)[:, None]], 1
    )


def combine(own_coeffs, pair_coeffs, side_bit, kron_zero, kron_one):
    kron_own = jnp.where(side_bit == 1, kron_one, kron_zero)
    kron_pair = jnp.where(side_bit == 1, kron_zero, kron_one)
    return SQRT_HALF * (apply_kron(own_coeffs, kron_own) + apply_kron(pair_coeffs, kron_pair))


def plain(positions, angles, weights, owner_dev, leaf_slot, phase_table):
    grid_order = Q
    points_sq = grid_order * grid_order
    wide_count = lax.axis_size("wide")
    narrow_count = lax.axis_size("narrow")
    devices = wide_count * narrow_count
    source_count = angles.shape[0]
    capacity = 4 * source_count // devices
    slot_count = devices * capacity
    box_count = phase_table.shape[1]
    target_dev = owner_dev[:, 0]
    dev_tags = jnp.arange(devices, dtype=jnp.int32)
    dev_counts = jnp.sum((target_dev[:, None] == dev_tags[None, :]).astype(jnp.int32), 0)
    dev_starts = jnp.cumsum(dev_counts) - dev_counts
    source_order = jnp.argsort(target_dev, stable=True)
    rank_grid = jnp.arange(capacity, dtype=jnp.int32)[None, :]
    slot_valid = (rank_grid < dev_counts[:, None]).reshape(slot_count)
    slot_pick = jnp.minimum(dev_starts[:, None] + rank_grid, source_count - 1).reshape(slot_count)
    slot_source = jnp.take(source_order, slot_pick, axis=0)
    records = jnp.stack([positions[0], positions[1], angles, weights])
    float_send = jnp.where(slot_valid[None, :], jnp.take(records, slot_source, axis=1), 0.0)
    index_send = jnp.where(slot_valid, jnp.take(leaf_slot, slot_source, axis=0), 0)[None, :]
    float_recv, index_recv = (
        lax.all_to_all(float_send, ("wide", "narrow"), split_axis=1, concat_axis=1, tiled=True),
        lax.all_to_all(index_send, ("wide", "narrow"), split_axis=1, concat_axis=1, tiled=True),
    )
    block_rows = math.gcd(slot_count, 2048)
    box_tags = jnp.arange(box_count, dtype=jnp.int32)

    def add_block(block_no, running):
        start = block_no * block_rows
        block_recs = lax.dynamic_slice_in_dim(float_recv, start, block_rows, 1)
        block_ids = lax.dynamic_slice_in_dim(index_recv[0], start, block_rows, 0)
        term_rows = leaf_terms(
            block_recs[0], block_recs[1], block_recs[2], block_recs[3], grid_order
        )
        one_hot = (block_ids[:, None] == box_tags[None, :]).astype(jnp.float32)
        return running + lax.dot_general(
            one_hot,
            term_rows,
            (((0,), (0,)), ((), ())),
            precision=HIGH,
            preferred_element_type=jnp.float32,
        )

    coeffs = lax.fori_loop(
        0, slot_count // block_rows, add_block, jnp.zeros((box_count, 2 * points_sq), jnp.float32)
    )
    kron_zero = interp_kron(grid_order, 0.0)
    kron_one = interp_kron(grid_order, 1.0)
    narrow_index = lax.axis_index("narrow")
    wide_index = lax.axis_index("wide")
    for bit_index in (0, 1):
        side_bit = jnp.bitwise_and(jnp.right_shift(narrow_index, bit_index), 1)
        rotated = rotate(coeffs, phase_table[bit_index])
        partner = partner_2(rotated, "narrow", bit_index)
        coeffs = combine(rotated, partner, side_bit, kron_zero, kron_one)
    top_bit = wide_count.bit_length() - 2
    for level_no, bit_index in ((2, 0), (3, 1), (4, top_bit)):
        side_bit = jnp.bitwise_and(jnp.right_shift(wide_index, bit_index), 1)
        rotated = rotate(coeffs, phase_table[level_no])
        partner = partner_2(rotated, "wide", bit_index)
        coeffs = combine(rotated, partner, side_bit, kron_zero, kron_one)
    return coeffs


NODES = np.cos((2 * np.arange(Q) + 1) * np.pi / (2 * Q))
GAPS = np.prod(NODES[:, None] - NODES[None, :] + np.eye(Q), 1)


def kron_table():
    blocks = []
    for side in (0.0, 1.0):
        points = (NODES + 2.0 * side - 1.0) * 0.5
        offsets = points[:, None] - NODES
        basis = np.stack(
            [np.prod(np.delete(offsets, k, 1), 1) / GAPS[k] for k in range(Q)], 1
        )
        blocks.append(np.kron(basis, basis).T)
    table = np.concatenate(blocks, 0) * SQRT_HALF
    high = table.astype(np.float32).astype(BF)
    low = (table - high.astype(np.float64)).astype(np.float32).astype(BF)
    return np.concatenate([high, high, low], 0)


def series(function, degree):
    fit = np.polynomial.chebyshev.Chebyshev.interpolate(
        lambda t: function(np.sqrt(t)), degree, domain=[0.0, np.pi**2]
    )
    return [float(c) for c in fit.convert(kind=np.polynomial.Polynomial).coef]


COS_SERIES = series(np.cos, 6)
SIN_SERIES = series(lambda x: np.sinc(x / np.pi), 6)


def cos_sin(angle):
    square = angle * angle
    cosine = jnp.full_like(angle, COS_SERIES[-1])
    for c in COS_SERIES[-2::-1]:
        cosine = cosine * square + c
    sine = jnp.full_like(angle, SIN_SERIES[-1])
    for c in SIN_SERIES[-2::-1]:
        sine = sine * square + c
    return cosine, sine * angle


def basis_rows(points):
    offsets = [points - float(t) for t in NODES]
    before = [None, offsets[0]]
    for k in range(1, Q - 1):
        before.append(before[-1] * offsets[k])
    after = [None, offsets[Q - 1]]
    for k in range(Q - 2, 0, -1):
        after.append(after[-1] * offsets[k])
    after = after[::-1]
    rows = []
    for k in range(Q):
        scale = float(1.0 / GAPS[k])
        if k == 0:
            rows.append(after[0] * scale)
        elif k == Q - 1:
            rows.append(before[k] * scale)
        else:
            rows.append(before[k] * after[k] * scale)
    return rows


def split(value, count):
    parts = []
    for _ in range(count - 1):
        part = value.astype(BF).astype(F32)
        parts.append(part)
        value = value - part
    return parts + [value]


def move_bits(value, table):
    out = None
    for source, target in table:
        bit = lax.shift_left(
            lax.bitwise_and(lax.shift_right_logical(value, jnp.int32(source)), jnp.int32(1)),
            jnp.int32(target),
        )
        out = bit if out is None else lax.bitwise_or(out, bit)
    return out


def move_bits_of(number, table):
    return sum(((number >> source) & 1) << target for source, target in table)


def group_bits(table):
    return tuple((step - 3, bit) for step, bit in table if step >= 3)


def group_row_bits(table):
    return tuple((step, dict(ROW_BITS)[bit]) for step, bit in group_bits(table))


def dot_nt(left, right):
    return lax.dot_general(left, right, (((1,), (1,)), ((), ())), preferred_element_type=F32)


def dot_nn(left, right):
    return jnp.dot(left, right, preferred_element_type=F32)


def body(
    pos_h, ang_h, wgt_h, own_h, slot_h, phase_h, all_h,
    out, flag,
    pos, ang, wgt, own, slot, phase, all_k, load_sem,
    pair_s, box_s, wc_s, ws_s, left_a, left_b, right_a, right_b, packed_s,
    send_rec, recv_rec, send_ph, recv_ph, send_out,
    basis_v, basis_c, basis_s, terms_s, hot_s, leaf_s, state_s, angle_s,
    rec_send, rec_recv, ph_send, ph_recv, out_send, out_recv, own_sem,
):
    me = lax.axis_index("wide") * 8 + lax.axis_index("narrow")
    my_row = move_bits(me, ROW_BITS)

    def device(t):
        return {"wide": lax.shift_right_logical(t, 3), "narrow": lax.bitwise_and(t, 7)}

    def for_partners(act, table=STEP_BITS):
        def visit(group, first):
            base = me if first else lax.bitwise_xor(me, move_bits(group, group_bits(table)))
            base_row = (
                my_row
                if first
                else lax.bitwise_xor(my_row, move_bits(group, group_row_bits(table)))
            )
            for j in range(1 if first else 0, GROUP):
                offset = move_bits_of(j, table)
                act(
                    group,
                    j,
                    lax.bitwise_xor(base, offset),
                    lax.bitwise_xor(base_row, move_bits_of(offset, ROW_BITS)),
                )

        visit(0, True)

        def later(group, carry):
            visit(group, False)
            return carry

        lax.fori_loop(1, GROUPS, later, 0)

    loads = [
        pltpu.make_async_copy(source, target, load_sem.at[i])
        for i, (source, target) in enumerate(
            (
                (phase_h, phase),
                (pos_h, pos),
                (ang_h, ang),
                (wgt_h, wgt),
                (own_h, own),
                (slot_h, slot),
                (all_h, all_k),
            )
        )
    ]
    for load in loads:
        load.start()

    barrier = pltpu.get_barrier_semaphore()

    def greet(group, j, t, row):
        pl.semaphore_signal(barrier, inc=1, device_id=device(t), device_id_type=MESH)

    for_partners(greet)

    def rows_of(block, count):
        first = block * 8
        return pl.ds(first if isinstance(first, int) else pl.multiple_of(first, 8), count)

    for load in loads[1:6]:
        load.wait()

    slots = slot[...]
    pair_s[...] = lax.shift_right_logical(slots, 1)
    box_s[...] = (
        move_bits(own[...], ROW_BITS) * 2 + lax.bitwise_and(slots, 1)
    ).astype(F32)
    cosine, sine = cos_sin(ang[...])
    gain = wgt[...] * LEAF_GAIN
    wc_s[...] = gain * cosine
    ws_s[...] = gain * sine
    packed_s[...] = jnp.zeros_like(packed_s)

    row_128 = lax.broadcasted_iota(jnp.int32, (128, LANES), 0)
    row_64 = lax.broadcasted_iota(jnp.int32, (64, LANES), 0).astype(F32).astype(BF)
    row_256 = lax.broadcasted_iota(jnp.int32, (256, LANES), 0).astype(F32).astype(BF)
    one, zero = jnp.asarray(1.0, BF), jnp.asarray(0.0, BF)
    before = lax.broadcasted_iota(jnp.int32, (LANES, 256), 0)
    column = lax.broadcasted_iota(jnp.int32, (LANES, 256), 1)
    counter = jnp.where((before < column) | (column >= LANES), 1.0, 0.0).astype(BF)

    def lay_out(block, left, right, counts):
        for j in range(STEP):
            c = block * STEP + j
            lanes = slice(j * LANES, (j + 1) * LANES)
            pair = pair_s[pl.ds(c, 1), :]
            named = row_128 == pair
            seen = dot_nn(jnp.where(named, 1.0, 0.0).astype(BF), counter)
            rank = jnp.sum(
                jnp.where(named, seen[:, :LANES] + counts, 0.0), axis=0, keepdims=True
            )
            counts = counts + seen[:, LANES:]
            high_pair = lax.shift_right_logical(pair, 6).astype(F32) * RANKS
            place = jnp.where(rank < RANKS, high_pair + rank, -1.0)
            right[:, lanes] = jnp.where(row_256 == place.astype(BF), one, zero)
            low_pair = row_64 == lax.bitwise_and(pair, 63).astype(F32).astype(BF)
            start = pl.multiple_of(c * LANES, LANES)
            values = (
                split(pos[0:1, pl.ds(start, LANES)], 3)
                + split(pos[1:2, pl.ds(start, LANES)], 3)
                + split(wc_s[pl.ds(c, 1), :], 2)
                + split(ws_s[pl.ds(c, 1), :], 2)
                + [box_s[pl.ds(c, 1), :]]
            )
            for p, value in enumerate(values):
                left[p * 64 : (p + 1) * 64, lanes] = jnp.where(low_pair, value.astype(BF), zero)
        return counts

    def gather(left, right):
        packed_s[...] += dot_nt(left[...], right[...])

    def two_blocks(pair, counts):
        counts = lay_out(2 * pair, left_a, right_a, counts)
        gather(left_b, right_b)
        counts = lay_out(2 * pair + 1, left_b, right_b, counts)
        gather(left_a, right_a)
        return counts

    left_b[...] = jnp.zeros_like(left_b)
    right_b[...] = jnp.zeros_like(right_b)
    counts = lax.fori_loop(0, BLOCKS // 2, two_blocks, jnp.zeros((128, LANES), F32))
    gather(left_b, right_b)
    too_many = jnp.max(jnp.max(counts, axis=0, keepdims=True), axis=1, keepdims=True)
    part = 0
    for field, count in enumerate((3, 3, 2, 2, 1)):
        value = packed_s[part * 64 : (part + 1) * 64, :]
        for extra in range(1, count):
            value = value + packed_s[(part + extra) * 64 : (part + extra + 1) * 64, :]
        if field == 0:
            value = jnp.where(too_many > RANKS, 4.0, value)
        part += count
        for half in range(2):
            send_rec[pl.ds(half * 512 + field, 64, stride=8), :] = value[
                :, half * LANES : (half + 1) * LANES
            ]

    pl.semaphore_wait(barrier, DEVICES - 1)

    own_rec = pltpu.make_async_copy(
        send_rec.at[pl.ds(pl.multiple_of(me * 8, 8), FIELDS)],
        recv_rec.at[pl.ds(0, FIELDS)],
        rec_recv.at[0],
    )
    own_rec.start()
    def send_records(group, j, t, row):
        pltpu.make_async_remote_copy(
            src_ref=send_rec.at[pl.ds(pl.multiple_of(t * 8, 8), FIELDS)],
            dst_ref=recv_rec.at[rows_of(group * GROUP + j, FIELDS)],
            send_sem=rec_send,
            recv_sem=rec_recv.at[group],
            device_id=device(t),
            device_id_type=MESH,
        ).start()

    for_partners(send_records)

    def send_phases(batch):
        levels = BATCHES[batch]

        def send(group, j, t, row):
            pltpu.make_async_remote_copy(
                src_ref=send_ph.at[levels, pl.ds(pl.multiple_of(t * 4, 4), 4)],
                dst_ref=recv_ph.at[levels, pl.ds(pl.multiple_of(my_row * 4, 4), 4)],
                send_sem=ph_send.at[batch],
                recv_sem=ph_recv.at[batch],
                device_id=device(t),
                device_id_type=MESH,
            ).start()

        for_partners(send, MIXED_BITS)

    loads[0].wait()
    for level in range(LEVELS):
        for k in range(2):
            send_ph[level, pl.ds(k, 256, stride=2), :] = phase[level, :, k * LANES : (k + 1) * LANES]

    own_ph = pltpu.make_async_copy(
        send_ph.at[:, pl.ds(pl.multiple_of(me * 4, 4), 4)],
        recv_ph.at[:, pl.ds(pl.multiple_of(my_row * 4, 4), 4)],
        own_sem.at[0],
    )
    own_ph.start()
    send_phases(0)

    def wait_for(ref, rows, sem):
        view = ref.at[pl.ds(0, rows)]
        pltpu.make_async_copy(view, view, sem).wait()

    def wait_phases(ref, batch, sems):
        view = ref.at[BATCHES[batch], pl.ds(0, (DEVICES - 1) * 4)]
        pltpu.make_async_copy(view, view, sems.at[batch]).wait()

    leaf_s[...] = jnp.zeros_like(leaf_s)

    def build(group, terms, hot, largest):
        first = pl.multiple_of(group * (GROUP * 8), GROUP * 8)
        field = [recv_rec[pl.ds(first + f, GROUP, stride=8), :] for f in range(FIELDS)]
        for k, value in enumerate(basis_rows(field[1])):
            basis_v[k * GROUP : (k + 1) * GROUP, :] = value
        for k, value in enumerate(basis_rows(field[0])):
            basis_c[k * GROUP : (k + 1) * GROUP, :] = value * field[2]
            basis_s[k * GROUP : (k + 1) * GROUP, :] = value * field[3]
        for s in range(GROUP):
            lanes = slice(s * LANES, (s + 1) * LANES)
            after = slice((GROUP + s) * LANES, (GROUP + s + 1) * LANES)
            second = basis_v[pl.ds(s, Q, stride=GROUP), :]
            for half, basis in enumerate((basis_c, basis_s)):
                for i in range(Q):
                    rows_i = slice(half * POINTS + i * Q, half * POINTS + (i + 1) * Q)
                    term = basis[i * GROUP + s : i * GROUP + s + 1, :] * second
                    high = term.astype(BF)
                    terms[rows_i, lanes] = high
                    terms[rows_i, after] = (term - high.astype(F32)).astype(BF)
            hot[:, lanes] = jnp.where(row_256 == field[4][s : s + 1, :].astype(BF), one, zero)
        return jnp.maximum(largest, field[0])

    def one_group(group, largest):
        wait_for(recv_rec, GROUP * FIELDS, rec_recv.at[group])
        largest = build(group, terms_s, hot_s, largest)
        width = GROUP * LANES
        leaf_s[...] += dot_nt(terms_s[:, :width], hot_s[...]) + dot_nt(
            terms_s[:, width:], hot_s[...]
        )
        return largest

    largest = lax.fori_loop(0, GROUPS, one_group, jnp.zeros((GROUP, LANES), F32))
    flag[0, 0] = jnp.max(largest)
    for load in loads[6:]:
        load.wait()
    state_s[...] = leaf_s[...].T

    own_ph.wait()

    def one_level(level, carry):
        for batch, levels in enumerate(BATCHES):

            @pl.when(level == levels.start)
            def _():
                wait_phases(recv_ph, batch, ph_recv)

        for tile in range(32):
            turned = lax.bitwise_and(
                lax.bitwise_or(
                    lax.shift_right_logical(jnp.int32(tile), level),
                    lax.shift_left(jnp.int32(tile), LEVELS - level),
                ),
                31,
            )
            for k in range(2):
                angle_s[tile * 8 : (tile + 1) * 8, k * LANES : (k + 1) * LANES] = recv_ph[
                    level, pl.ds(turned * 16 + k, 8, stride=2), :
                ]
        cosine, sine = cos_sin(angle_s[...])
        real, imag = state_s[:, :POINTS], state_s[:, POINTS:]
        both = []
        for value in (cosine * real - sine * imag, sine * real + cosine * imag):
            both.append(jnp.concatenate([value[:128], value[128:]], axis=1))
        both = jnp.concatenate(both, axis=0)
        high = both.astype(BF)
        low = (both - high.astype(F32)).astype(BF)
        new = dot_nn(jnp.concatenate([high, low, high], axis=1), all_k[...])
        for half in range(2):
            part_new = new[half * 128 : (half + 1) * 128].reshape(16, 1, 8, POINTS)
            state_s[:, half * POINTS : (half + 1) * POINTS] = jnp.broadcast_to(
                part_new, (16, 2, 8, POINTS)
            ).reshape(256, POINTS)
        return carry

    lax.fori_loop(0, LEVELS, one_level, 0)

    for k in range(4):
        send_out[pl.ds(k, 256, stride=4), :] = state_s[:, k * LANES : (k + 1) * LANES]
    own_out = pltpu.make_async_copy(
        send_out.at[pl.ds(pl.multiple_of(my_row * 8, 8), 8)],
        out.at[pl.ds(pl.multiple_of(me * 8, 8), 8)],
        own_sem.at[1],
    )
    own_out.start()

    def send_results(group, j, t, row):
        pltpu.make_async_remote_copy(
            src_ref=send_out.at[rows_of(row, 8)],
            dst_ref=out.at[pl.ds(pl.multiple_of(me * 8, 8), 8)],
            send_sem=out_send,
            recv_sem=out_recv,
            device_id=device(t),
            device_id_type=MESH,
        ).start()

    for_partners(send_results, MIXED_BITS)
    own_out.wait()
    wait_for(out, (DEVICES - 1) * 8, out_recv)
    wait_for(send_rec, (DEVICES - 1) * FIELDS, rec_send)
    for batch in range(len(BATCHES)):
        wait_phases(send_ph, batch, ph_send)
    wait_for(send_out, (DEVICES - 1) * 8, out_send)


def fast(positions, angles, weights, owner_dev, leaf_slot, phase_table):
    dma = pltpu.SemaphoreType.DMA
    return pl.pallas_call(
        body,
        out_shape=(
            jax.ShapeDtypeStruct((1024, LANES), F32),
            jax.ShapeDtypeStruct((1, 1), F32),
        ),
        in_specs=[pl.BlockSpec(memory_space=pl.ANY)] * 7,
        out_specs=(
            pl.BlockSpec(memory_space=pl.ANY),
            pl.BlockSpec(memory_space=pltpu.SMEM),
        ),
        scratch_shapes=[
            pltpu.VMEM((2, SOURCES), F32),
            pltpu.VMEM((64, LANES), F32),
            pltpu.VMEM((64, LANES), F32),
            pltpu.VMEM((64, LANES), jnp.int32),
            pltpu.VMEM((64, LANES), jnp.int32),
            pltpu.VMEM((LEVELS, 256, POINTS), F32),
            pltpu.VMEM((1536, POINTS), BF),
            dma((7,)),
            pltpu.VMEM((64, LANES), jnp.int32),
            pltpu.VMEM((64, LANES), F32),
            pltpu.VMEM((64, LANES), F32),
            pltpu.VMEM((64, LANES), F32),
            pltpu.VMEM((PARTS * 64, STEP * LANES), BF),
            pltpu.VMEM((PARTS * 64, STEP * LANES), BF),
            pltpu.VMEM((256, STEP * LANES), BF),
            pltpu.VMEM((256, STEP * LANES), BF),
            pltpu.VMEM((PARTS * 64, 256), F32),
            pltpu.VMEM((1024, LANES), F32),
            pltpu.VMEM((1024, LANES), F32),
            pltpu.VMEM((LEVELS, 512, LANES), F32),
            pltpu.VMEM((LEVELS, 512, LANES), F32),
            pltpu.VMEM((1024, LANES), F32),
            pltpu.VMEM((Q * GROUP, LANES), F32),
            pltpu.VMEM((Q * GROUP, LANES), F32),
            pltpu.VMEM((Q * GROUP, LANES), F32),
            pltpu.VMEM((512, 2 * GROUP * LANES), BF),
            pltpu.VMEM((256, GROUP * LANES), BF),
            pltpu.VMEM((512, 256), F32),
            pltpu.VMEM((256, 512), F32),
            pltpu.VMEM((256, POINTS), F32),
            dma,
            dma((GROUPS,)),
            dma((len(BATCHES),)),
            dma((len(BATCHES),)),
            dma,
            dma,
            dma((2,)),
        ],
        compiler_params=pltpu.CompilerParams(
            collective_id=0, has_side_effects=True, vmem_limit_bytes=56 << 20
        ),
    )(
        positions,
        angles.reshape(64, LANES),
        weights.reshape(64, LANES),
        owner_dev.reshape(64, LANES),
        leaf_slot.reshape(64, LANES),
        phase_table,
        jnp.asarray(kron_table()),
    )


def shards(*arrays):
    result, largest = fast(*arrays)
    return lax.cond(
        largest[0, 0] > 2.0, plain, lambda *_: result.reshape(256, 512), *arrays
    )


def solution(mesh):
    placed = (
        P(None, ("wide", "narrow")),
        P(("wide", "narrow")),
        P(("wide", "narrow")),
        P(("wide", "narrow"), None),
        P(("wide", "narrow")),
        P(None, ("wide", "narrow"), None),
    )
    return jax.shard_map(
        shards, mesh=mesh, in_specs=placed, out_specs=P(("wide", "narrow"), None), check_vma=False
    )
```
